256 devices in a mesh: pop: 32 (over y_hi, z, core), col: 8 (over y_lo, x).
Axes of the slice: x: 4, y: 4 (y_hi: 2, y_lo: 2; y = y_hi * 2 + y_lo), z: 8, core: 2. Of those that a mesh axis runs over, the one named last changes fastest.
Arguments:
- states: bfloat16 [32768, 2048], P('pop', 'col'), may hold values from -6 to 6
- weight: bfloat16 [2048, 2048], P(None, 'col'), may hold values from -0.125 to 0.125
- noise_in: bfloat16 [32768, 2048], P('pop', 'col'), may hold values from -6 to 6
- noise_out: bfloat16 [32768, 2048], P('pop', 'col'), may hold values from -6 to 6
- fitness: float32 [32768], P('pop'), may hold values from -50 to 50
Outputs:
- final_states: bfloat16 [32768, 2048], P('pop', 'col')
- update: float32 [2048, 2048], P('pop', 'col')
The draws below stay inside these ranges and needn't reach their ends.
All inputs are finite; a program needn't handle non-finite values.
Results may differ from the reference program's by a relative error of at most 0.014.
Values may be sent and summed in bfloat16 or wider, within the bound.
No kernel may reach another device: no remote copies, remote signals or barrier semaphores. Data moves between devices by JAX's collectives and lax.ppermute only.
A program may use at most 64 MiB of HBM per device.

```python
import jax
import jax.numpy as jnp
from jax import lax

D = 2048
MEM_DEV = 1024
STEPS = 4
POP = 32768


def draw_fitness(key, part):
    key = jax.random.fold_in(key, 7)
    base_key = jax.random.fold_in(key, 1)
    block_key = jax.random.fold_in(key, 2)
    position = jnp.arange(POP, dtype=jnp.float32) / max(POP - 1, 1)
    blocks = POP // MEM_DEV
    offsets = jax.random.uniform(block_key, (blocks,), jnp.float32, -10.0, 10.0)
    shifted = jnp.repeat(offsets, MEM_DEV, total_repeat_length=POP)
    rising = jnp.exp(jnp.log(3.0) * position)
    base = jax.random.normal(base_key, (POP,), jnp.float32) + 1.0
    return jnp.clip(rising * base + shifted, -50.0, 50.0)


def levels(stream_key, dims, split, low, high):
    loudness, own = 1.0, jax.random.fold_in(stream_key, 6)
    for dim, shards_of in split:
        draws = jnp.exp(jax.random.uniform(jax.random.fold_in(own, dim), (shards_of,), jnp.float32, low / len(split), high / len(split)))
        loudness = loudness * jnp.repeat(draws, dims[dim] // shards_of).reshape([-1 if axis == dim else 1 for axis in range(len(dims))])
    return loudness


def noise(own_key, dims, spread, limit, split=(), kind=jnp.bfloat16):
    array = jax.random.normal(own_key, dims, jnp.float32) * spread
    if len(split) > 0:
        array = levels(own_key, dims, split, -0.22, 0.18) * array
    return jnp.clip(array, min=-limit, max=limit).astype(kind)


def setup_inputs(seed: int = 0) -> dict:
    arg_keys = jax.random.split(jax.random.key(seed), 6)
    states = noise(arg_keys[0], (POP, D), 1.0, 6.0, ((0, 32), (1, 8)))
    weight = noise(arg_keys[1], (D, D), D ** -0.5, 0.125, ((1, 8),))
    noise_in = noise(arg_keys[2], (POP, D), 1.0, 6.0, ((0, 32), (1, 8)))
    noise_out = noise(arg_keys[3], (POP, D), 1.0, 6.0, ((0, 32), (1, 8)))
    fitness = draw_fitness(jax.random.fold_in(arg_keys[5], 71), 0)
    return dict(states=states, weight=weight, noise_in=noise_in, noise_out=noise_out, fitness=fitness)


noise_scale = 0.02

def reference(states, weight, noise_in, noise_out, fitness):
    x = states
    a32 = noise_in.astype(jnp.float32)
    b32 = noise_out.astype(jnp.float32)
    for step in range(STEPS):
        dots = lax.optimization_barrier(jnp.sum(x.astype(jnp.float32) * a32, axis=1))
        pre = jnp.dot(x, weight, preferred_element_type=jnp.float32) + noise_scale * dots[:, None] * b32
        x = jnp.tanh(pre).astype(jnp.bfloat16)
    mean = jnp.sum(fitness) / POP
    var = jnp.sum((fitness - mean) ** 2) / POP
    normed = (fitness - mean) / jnp.sqrt(var + 1e-05)
    scaled = (normed[:, None] * a32).astype(jnp.bfloat16)
    update = jnp.dot(scaled.T, noise_out, preferred_element_type=jnp.float32) / jnp.sqrt(jnp.float32(POP))
    return (x, update)
```

```python
import functools

import jax
import jax.numpy as jnp
from jax import lax
from jax.experimental import pallas as pl
from jax.experimental.pallas import tpu as pltpu
from jax.sharding import Mesh, PartitionSpec as P

STEPS = 4
SCALE = 0.02
POP = 32768
POP_AXES = ("yh", "z", "c")
COL_AXES = ("yl", "x")
SHIFTS = [(dy, dx) for dy in range(2) for dx in range(4)]
BF = jnp.bfloat16
F32 = jnp.float32


def col_shift(v, dy, dx):
    perm = []
    for yl in range(2):
        for x in range(4):
            perm.append((yl * 4 + x, (yl ^ dy) * 4 + (x + dx) % 4))
    return lax.ppermute(v, COL_AXES, perm)


def z_shift(v, d):
    return lax.ppermute(v, "z", [(i, (i + d) % 8) for i in range(8)])


def swap(v, axis):
    return lax.ppermute(v, axis, [(0, 1), (1, 0)])


def members_kernel(pos_ref, s_ref, a_ref, b_ref, *rest):
    outs, sem = rest[:8], rest[8]
    copies = []
    for k in range(8):
        rows = pl.ds(pl.multiple_of(pos_ref[k] * 128, 128), 128)
        for n, src in enumerate((s_ref, a_ref, b_ref)):
            copies.append(pltpu.make_async_copy(src.at[rows], outs[k].at[n], sem.at[3 * k + n]))
    for cp in copies:
        cp.start()
    for cp in copies:
        cp.wait()


def split_members(pos, states, a, b):
    return pl.pallas_call(
        members_kernel,
        out_shape=[jax.ShapeDtypeStruct((3, 128, 256), BF)] * 8,
        in_specs=[pl.BlockSpec(memory_space=pltpu.SMEM)] + [pl.BlockSpec(memory_space=pl.ANY)] * 3,
        out_specs=[pl.BlockSpec(memory_space=pl.ANY)] * 8,
        scratch_shapes=[pltpu.SemaphoreType.DMA((24,))],
        name="split_members",
    )(pos, states, a, b)


def rollout_kernel(n_whole, pos_ref, *refs):
    n_w = len(refs) - 8 - 1 - 5
    pieces, members = refs[:n_w], refs[n_w:n_w + 8]
    out_ref = refs[n_w + 8]
    w, m, x, pre, sem = refs[n_w + 9:]
    copies = []
    for k in range(8):
        copies.append(pltpu.make_async_copy(members[k], m.at[:, :, k * 256:(k + 1) * 256], sem.at[k]))
    for i in range(n_w):
        rows = pl.ds(pl.multiple_of(pos_ref[i] * 128, 128), 128)
        if i < n_whole:
            cols = slice(0, 8)
        else:
            cols = slice(0, 4) if (i - n_whole) % 2 == 0 else slice(4, 8)
        copies.append(pltpu.make_async_copy(pieces[i], w.at[cols, rows], sem.at[8 + i]))
    for cp in copies:
        cp.start()
    for cp in copies:
        cp.wait()
    x[...] = m[0]

    def step(_, carry):
        cur = x[...]
        dots = jnp.sum(cur.astype(F32) * m[1].astype(F32), axis=1, keepdims=True)
        gain = SCALE * dots
        for r in range(8):
            pre[:, r * 256:(r + 1) * 256] = jnp.dot(cur, w[r], preferred_element_type=F32)
        for r in range(8):
            c = slice(r * 256, (r + 1) * 256)
            x[:, c] = jnp.tanh(pre[:, c] + gain * m[2, :, c].astype(F32)).astype(BF)
        return carry

    lax.fori_loop(0, STEPS, step, 0)
    for r in range(8):
        out_ref[r] = x[:, r * 256:(r + 1) * 256]


def rollout(pos, whole, halves, members):
    pieces = whole + halves
    n = len(pieces)
    return pl.pallas_call(
        functools.partial(rollout_kernel, len(whole)),
        out_shape=jax.ShapeDtypeStruct((8, 128, 256), BF),
        in_specs=[pl.BlockSpec(memory_space=pltpu.SMEM)] + [pl.BlockSpec(memory_space=pl.ANY)] * (n + 8),
        out_specs=pl.BlockSpec(memory_space=pltpu.VMEM),
        scratch_shapes=[
            pltpu.VMEM((8, 2048, 256), BF),
            pltpu.VMEM((3, 128, 2048), BF),
            pltpu.VMEM((128, 2048), BF),
            pltpu.VMEM((128, 2048), F32),
            pltpu.SemaphoreType.DMA((8 + n,)),
        ],
        compiler_params=pltpu.CompilerParams(vmem_limit_bytes=32 * 2**20),
        cost_estimate=pl.CostEstimate(flops=2 * 128 * 2048 * 2048 * 4, bytes_accessed=10 * 2**20, transcendentals=2**20),
        name="rollout",
    )(pos, *pieces, *members)


def update_kernel(pos_ref, norm_ref, a0, a1, a2, a3, b0, b1, keep_ref, send_ref):
    c = pos_ref[4]
    first = c == 0
    for k, a in enumerate((a0, a1, a2, a3)):
        xb = pos_ref[k]
        scaled = (norm_ref[...] * a[...].astype(F32)).astype(BF)
        for h, b in enumerate((b0, b1)):
            d = lax.dot_general(scaled, b[...], (((0,), (0,)), ((), ())), preferred_element_type=F32)
            d = d.reshape(2, 2, 64, 256)
            cols = slice(h * 256, (h + 1) * 256)
            keep_ref[pl.ds(2 * xb, 2), :, cols] = jnp.where(first, d[:, 0], d[:, 1])
            send_ref[pl.ds(2 * xb, 2), :, cols] = jnp.where(first, d[:, 1], d[:, 0])


def partial_update(pos, norm, a, b):
    shape = jax.ShapeDtypeStruct((8, 64, 512), F32)
    return pl.pallas_call(
        update_kernel,
        out_shape=[shape, shape],
        in_specs=[pl.BlockSpec(memory_space=pltpu.SMEM)] + [pl.BlockSpec(memory_space=pltpu.VMEM)] * 7,
        out_specs=[pl.BlockSpec(memory_space=pltpu.VMEM)] * 2,
        compiler_params=pltpu.CompilerParams(vmem_limit_bytes=32 * 2**20),
        cost_estimate=pl.CostEstimate(flops=2 * 1024 * 1024 * 512, bytes_accessed=6 * 2**20, transcendentals=0),
        name="partial_update",
    )(pos, norm, *a, *b)


def join_kernel(pos_ref, *refs):
    pieces, out_ref, sem = refs[:8], refs[8], refs[9]
    copies = []
    for k in range(8):
        rows = pl.ds(pl.multiple_of(pos_ref[k] * 128, 128), 128)
        copies.append(pltpu.make_async_copy(pieces[k], out_ref.at[rows], sem.at[k]))
    for cp in copies:
        cp.start()
    for cp in copies:
        cp.wait()


def join_members(pos, pieces):
    return pl.pallas_call(
        join_kernel,
        out_shape=jax.ShapeDtypeStruct((1024, 256), BF),
        in_specs=[pl.BlockSpec(memory_space=pltpu.SMEM)] + [pl.BlockSpec(memory_space=pl.ANY)] * 8,
        out_specs=pl.BlockSpec(memory_space=pl.ANY),
        scratch_shapes=[pltpu.SemaphoreType.DMA((8,))],
        name="join_members",
    )(pos, *pieces)


def local(states, weight, noise_in, noise_out, fitness):
    yh, z, c = (lax.axis_index(n) for n in POP_AXES)
    yl, x = (lax.axis_index(n) for n in COL_AXES)

    with jax.named_scope("weight_rows"):
        share = lax.dynamic_slice_in_dim(weight, z * 256 + c * 128, 128, 0)
        shares = [share] + [col_shift(share, dy, dx) for dy, dx in SHIFTS[1:]]
        own = jnp.stack(shares)

    with jax.named_scope("weight_ring"):
        ring = {0: own}
        for d in (1, 2, 3):
            ring[d] = z_shift(ring[d - 1], 1)
            ring[-d] = z_shift(ring[1 - d], -1)
        last = [z_shift(ring[3][:4], 1), z_shift(ring[-3][4:], -1)]
        order = [0, 1, -1, 2, -2, 3, -3]
        whole, halves, wpos = [], [], []

        def row_block(zz, cc):
            dy = (zz // 4) ^ yl
            dx = (x - zz) % 4
            return (dy * 4 + dx) * 2 + cc

        for d in order:
            whole += [ring[d], swap(ring[d], "c")]
            wpos += [row_block((z - d) % 8, c), row_block((z - d) % 8, 1 - c)]
        for cc, part in ((c, last), (1 - c, [swap(v, "c") for v in last])):
            halves += part
            wpos += [row_block((z + 4) % 8, cc)] * 2
        wpos = jnp.stack(wpos).astype(jnp.int32)

    with jax.named_scope("members"):
        to = jnp.stack([(yl ^ dy) * 4 + (x + dx) % 4 for dy, dx in SHIFTS]).astype(jnp.int32)
        parts = split_members(to, states, noise_in, noise_out)
        members = [parts[0]] + [col_shift(v, dy, dx) for v, (dy, dx) in zip(parts[1:], SHIFTS[1:])]

    with jax.named_scope("fitness"):
        spread = jnp.broadcast_to(fitness.reshape(1, 8, 128), (32, 8, 128))
        everyone = lax.all_to_all(spread, POP_AXES, 0, 0)
        mean = jnp.sum(everyone) / POP
        var = jnp.sum((everyone - mean) ** 2) / POP
        normed = (fitness - mean) / jnp.sqrt(var + 1e-05)

    with jax.named_scope("update"):
        a = [noise_in] + [
            lax.ppermute(noise_in, "x", [(i, (i + dx) % 4) for i in range(4)]) for dx in (1, 2, 3)
        ]
        b = [noise_out, swap(noise_out, "yl")]
        upos = jnp.stack([(x - dx) % 4 for dx in range(4)] + [c]).astype(jnp.int32)
        keep, send = partial_update(upos, normed.reshape(1024, 1), a, b)
        both = (keep + swap(send, "c")).astype(BF)
        stacked = lax.all_to_all(both, "z", 0, 0)
        total = jnp.sum(stacked.astype(F32), axis=0)
        left, right = total[:, :256], total[:, 256:]
        same = yh == yl
        one = jnp.where(same, left, right)
        two = jnp.where(same, right, left)
        pairs = [(i, j) for i in range(2) for j in range(2)]
        one = lax.ppermute(one, ("yh", "yl"), [(i * 2 + j, j * 2 + i) for i, j in pairs])
        two = lax.ppermute(two, ("yh", "yl"), [(i * 2 + j, j * 2 + (1 - i)) for i, j in pairs])
        update = (one + two) / jnp.sqrt(jnp.float32(POP))

    with jax.named_scope("rollout"):
        done = rollout(wpos, whole, halves, members)
    with jax.named_scope("states_back"):
        back = [done[0]] + [col_shift(done[k], dy, -dx) for k, (dy, dx) in enumerate(SHIFTS) if k > 0]
        final = join_members(to, back)
    return final, update


def solution(mesh):
    fine = Mesh(mesh.devices.reshape(2, 8, 2, 2, 4), POP_AXES + COL_AXES)
    both = P(POP_AXES, COL_AXES)
    return jax.shard_map(
        local,
        mesh=fine,
        in_specs=(both, P(None, COL_AXES), both, both, P(POP_AXES)),
        out_specs=(both, both),
        check_vma=False,
    )
```

```python
import functools

import jax
import jax.numpy as jnp
from jax import lax
from jax.experimental import pallas as pl
from jax.experimental.pallas import tpu as pltpu
from jax.sharding import Mesh, PartitionSpec as P

STEPS = 4
SCALE = 0.02
POP = 32768
POP_AXES = ("yh", "z", "c")
COL_AXES = ("yl", "x")
SHIFTS = [(dy, dx) for dy in range(2) for dx in range(4)]
BF = jnp.bfloat16
F32 = jnp.float32


def col_shift(v, dy, dx):
    perm = []
    for yl in range(2):
        for x in range(4):
            perm.append((yl * 4 + x, (yl ^ dy) * 4 + (x + dx) % 4))
    return lax.ppermute(v, COL_AXES, perm)


def z_shift(v, d):
    return lax.ppermute(v, "z", [(i, (i + d) % 8) for i in range(8)])


def swap(v, axis):
    return lax.ppermute(v, axis, [(0, 1), (1, 0)])


def after(v, *deps):
    return lax.optimization_barrier((v,) + deps)[0]


def split_kernel(pos_ref, s_ref, a_ref, b_ref, *outs):
    for k in range(8):
        rows = pl.ds(pl.multiple_of(pos_ref[k] * 128, 128), 128)
        for n, src in enumerate((s_ref, a_ref, b_ref)):
            outs[k][n] = src[rows, :]


def split_members(pos, states, a, b):
    return pl.pallas_call(
        split_kernel,
        out_shape=[jax.ShapeDtypeStruct((3, 128, 256), BF)] * 8,
        in_specs=[pl.BlockSpec(memory_space=pltpu.SMEM)] + [pl.BlockSpec(memory_space=pltpu.VMEM)] * 3,
        out_specs=[pl.BlockSpec(memory_space=pltpu.VMEM)] * 8,
        name="split_members",
    )(pos, states, a, b)


def rollout_kernel(pos_ref, *refs):
    n_w = len(refs) - 8 - 1 - 5
    pieces, members = refs[:n_w], refs[n_w:n_w + 8]
    out_ref = refs[n_w + 8]
    w, m, x, pre, sem = refs[n_w + 9:]
    copies = []
    for k in range(8):
        copies.append(pltpu.make_async_copy(members[k], m.at[:, :, k * 256:(k + 1) * 256], sem.at[k]))
    for i in range(n_w):
        rows = pl.ds(pl.multiple_of(pos_ref[i] * 256, 256), 256)
        cols = slice(0, 4) if i % 2 == 0 else slice(4, 8)
        copies.append(pltpu.make_async_copy(pieces[i], w.at[cols, rows], sem.at[8 + i]))
    for cp in copies:
        cp.start()
    for cp in copies:
        cp.wait()
    x[...] = m[0]

    def step(_, carry):
        cur = x[...]
        dots = jnp.sum(cur.astype(F32) * m[1].astype(F32), axis=1, keepdims=True)
        gain = SCALE * dots
        for r in range(8):
            pre[:, r * 256:(r + 1) * 256] = jnp.dot(cur, w[r], preferred_element_type=F32)
        for r in range(8):
            c = slice(r * 256, (r + 1) * 256)
            x[:, c] = jnp.tanh(pre[:, c] + gain * m[2, :, c].astype(F32)).astype(BF)
        return carry

    lax.fori_loop(0, STEPS, step, 0)
    for r in range(8):
        out_ref[r] = x[:, r * 256:(r + 1) * 256]


def rollout(pos, pieces, members):
    n = len(pieces)
    return pl.pallas_call(
        rollout_kernel,
        out_shape=jax.ShapeDtypeStruct((8, 128, 256), BF),
        in_specs=[pl.BlockSpec(memory_space=pltpu.SMEM)] + [pl.BlockSpec(memory_space=pl.ANY)] * (n + 8),
        out_specs=pl.BlockSpec(memory_space=pltpu.VMEM),
        scratch_shapes=[
            pltpu.VMEM((8, 2048, 256), BF),
            pltpu.VMEM((3, 128, 2048), BF),
            pltpu.VMEM((128, 2048), BF),
            pltpu.VMEM((128, 2048), F32),
            pltpu.SemaphoreType.DMA((8 + n,)),
        ],
        compiler_params=pltpu.CompilerParams(vmem_limit_bytes=60 * 2**20),
        cost_estimate=pl.CostEstimate(flops=2 * 128 * 2048 * 2048 * 4, bytes_accessed=10 * 2**20, transcendentals=2**20),
        name="rollout",
    )(pos, *pieces, *members)


def update_kernel(pos_ref, norm_ref, a0, a1, a2, a3, b0, b1, keep_ref, send_ref):
    c = pos_ref[4]
    first = c == 0
    for k, a in enumerate((a0, a1, a2, a3)):
        xb = pos_ref[k]
        scaled = (norm_ref[...] * a[...].astype(F32)).astype(BF)
        for h, b in enumerate((b0, b1)):
            d = lax.dot_general(scaled, b[...], (((0,), (0,)), ((), ())), preferred_element_type=F32)
            d = d.reshape(2, 2, 64, 256)
            cols = slice(h * 256, (h + 1) * 256)
            keep_ref[pl.ds(2 * xb, 2), :, cols] = jnp.where(first, d[:, 0], d[:, 1])
            send_ref[pl.ds(2 * xb, 2), :, cols] = jnp.where(first, d[:, 1], d[:, 0])


def partial_update(pos, norm, a, b):
    shape = jax.ShapeDtypeStruct((8, 64, 512), F32)
    return pl.pallas_call(
        update_kernel,
        out_shape=[shape, shape],
        in_specs=[pl.BlockSpec(memory_space=pltpu.SMEM)] + [pl.BlockSpec(memory_space=pltpu.VMEM)] * 7,
        out_specs=[pl.BlockSpec(memory_space=pltpu.VMEM)] * 2,
        compiler_params=pltpu.CompilerParams(vmem_limit_bytes=32 * 2**20),
        cost_estimate=pl.CostEstimate(flops=2 * 1024 * 1024 * 512, bytes_accessed=6 * 2**20, transcendentals=0),
        name="partial_update",
    )(pos, norm, *a, *b)


def join_kernel(pos_ref, *refs):
    pieces, out_ref = refs[:8], refs[8]
    for k in range(8):
        out_ref[pl.ds(pl.multiple_of(pos_ref[k] * 128, 128), 128), :] = pieces[k][...]


def join_members(pos, pieces):
    return pl.pallas_call(
        join_kernel,
        out_shape=jax.ShapeDtypeStruct((1024, 256), BF),
        in_specs=[pl.BlockSpec(memory_space=pltpu.SMEM)] + [pl.BlockSpec(memory_space=pltpu.VMEM)] * 8,
        out_specs=pl.BlockSpec(memory_space=pltpu.VMEM),
        name="join_members",
    )(pos, *pieces)


def local(states, weight, noise_in, noise_out, fitness):
    yh, z, c = (lax.axis_index(n) for n in POP_AXES)
    yl, x = (lax.axis_index(n) for n in COL_AXES)

    with jax.named_scope("weight_rows"):
        share = lax.dynamic_slice_in_dim(weight, (z % 4) * 512 + c * 256, 256, 0)
        shares = [share] + [col_shift(share, dy, dx) for dy, dx in SHIFTS[1:]]
        own = [jnp.stack(shares[:4]), jnp.stack(shares[4:])]

    to = jnp.stack([(yl ^ dy) * 4 + (x + dx) % 4 for dy, dx in SHIFTS]).astype(jnp.int32)
    with jax.named_scope("split"):
        parts = split_members(to, states, noise_in, noise_out)
    with jax.named_scope("fitness"):
        two = jnp.stack([fitness, swap(fitness, "c")])
        four = jnp.stack([two, swap(two, "yh")])

    with jax.named_scope("gather_a"):
        a_in, b_in = after((noise_in, noise_out), *own)
        a = [a_in] + [lax.ppermute(a_in, "x", [(i, (i + dx) % 4) for i in range(4)]) for dx in (1, 2, 3)]
        b = [b_in, swap(b_in, "yl")]

    with jax.named_scope("weight_ring"):
        def row_block(zz, cc):
            return ((zz // 2) ^ yl) * 4 + (x - zz * 2 - cc) % 4

        up = [z_shift(v, 1) for v in own]
        down = [z_shift(v, -1) for v in own]
        far = [z_shift(up[0], 1), z_shift(down[1], -1)]
        pieces, wpos = [], []
        for d, part in ((0, own), (1, up), (-1, down), (2, far)):
            for cc, vs in ((c, part), (1 - c, [swap(v, "c") for v in part])):
                pieces += vs
                wpos += [row_block((z - d) % 4, cc)] * 2
        wpos = jnp.stack(wpos).astype(jnp.int32)

    with jax.named_scope("members"):
        sent = after(tuple(parts[1:]), a[1])
        members = [parts[0]] + [col_shift(v, dy, dx) for v, (dy, dx) in zip(sent, SHIFTS[1:])]

    with jax.named_scope("fitness"):
        four = after(four, *own)
        everyone = lax.all_to_all(jnp.broadcast_to(four.reshape(1, 32, 128), (8, 32, 128)), "z", 0, 0)
        mean = jnp.sum(everyone) / POP
        var = jnp.sum((everyone - mean) ** 2) / POP
        normed = (fitness - mean) / jnp.sqrt(var + 1e-05)

    with jax.named_scope("update"):
        upos = jnp.stack([(x - dx) % 4 for dx in range(4)] + [c]).astype(jnp.int32)
        keep, send = partial_update(upos, normed.reshape(1024, 1), a, b)
        both = (keep + swap(send, "c")).astype(BF)
        stacked = lax.all_to_all(both, "z", 0, 0)
        total = jnp.sum(stacked.astype(F32), axis=0)
        left, right = total[:, :256], total[:, 256:]
        same = yh == yl
        one = jnp.where(same, left, right)
        two = jnp.where(same, right, left)
        pairs = [(i, j) for i in range(2) for j in range(2)]
        one = lax.ppermute(one, ("yh", "yl"), [(i * 2 + j, j * 2 + i) for i, j in pairs])
        two = lax.ppermute(two, ("yh", "yl"), [(i * 2 + j, j * 2 + (1 - i)) for i, j in pairs])
        update = (one + two) / jnp.sqrt(jnp.float32(POP))

    with jax.named_scope("rollout"):
        done = rollout(wpos, pieces, members)
    with jax.named_scope("states_back"):
        back = [done[0]] + [col_shift(done[k], dy, -dx) for k, (dy, dx) in enumerate(SHIFTS) if k > 0]
        final = join_members(to, back)
    return final, update


def solution(mesh):
    fine = Mesh(mesh.devices.reshape(2, 8, 2, 2, 4), POP_AXES + COL_AXES)
    both = P(POP_AXES, COL_AXES)
    return jax.shard_map(
        local,
        mesh=fine,
        in_specs=(both, P(None, COL_AXES), both, both, P(POP_AXES)),
        out_specs=(both, both),
        check_vma=False,
    )
```

```python
import jax
import jax.numpy as jnp
from jax import lax
from jax.experimental import pallas as pl
from jax.experimental.pallas import tpu as pltpu
from jax.sharding import Mesh, PartitionSpec as P

STEPS = 4
SCALE = 0.02
POP = 32768
POP_AXES = ("yh", "z", "c")
COL_AXES = ("yl", "x")
SHIFTS = [(dy, dx) for dx in range(4) for dy in range(2)]
BF = jnp.bfloat16
F32 = jnp.float32


def col_shift(v, dy, dx):
    perm = []
    for yl in range(2):
        for x in range(4):
            perm.append((yl * 4 + x, (yl ^ dy) * 4 + (x + dx) % 4))
    return lax.ppermute(v, COL_AXES, perm)


def shift(v, axis, d):
    n = 8 if axis == "z" else 4
    return lax.ppermute(v, axis, [(i, (i + d) % n) for i in range(n)])


def swap(v, axis):
    return lax.ppermute(v, axis, [(0, 1), (1, 0)])


def after(v, *deps):
    return lax.optimization_barrier((v,) + deps)[0]


def rows_of(block):
    return pl.ds(pl.multiple_of(block * 128, 128), 128)


def cost(us):
    return pl.CostEstimate(flops=int(us * 1.15e9), bytes_accessed=0, transcendentals=0)


def split_kernel(ids_ref, s_ref, b_ref, o_ref, out_ref):
    yl = ids_ref[3]
    for k in range(4):
        mine, other = rows_of(yl * 4 + k), rows_of((1 - yl) * 4 + k)
        out_ref[k, 0] = s_ref[mine, :]
        out_ref[k, 1] = s_ref[other, :]
        out_ref[k, 2] = b_ref[mine, :]
        out_ref[k, 3] = o_ref[mine, :]


def split_members(ids, states, b, other):
    return pl.pallas_call(
        split_kernel,
        out_shape=jax.ShapeDtypeStruct((4, 4, 128, 256), BF),
        in_specs=[pl.BlockSpec(memory_space=pltpu.SMEM)] + [pl.BlockSpec(memory_space=pltpu.VMEM)] * 3,
        out_specs=pl.BlockSpec(memory_space=pltpu.VMEM),
        compiler_params=pltpu.CompilerParams(vmem_limit_bytes=60 * 2**20),
        cost_estimate=cost(3),
        name="split_members",
    )(ids, states, b, other)


def pick_kernel(ids_ref, a_ref, own_ref, other_ref, sem):
    yl, x = ids_ref[3], ids_ref[4]
    copies = []
    for k in range(4):
        copies.append(pltpu.make_async_copy(a_ref.at[k, rows_of(yl * 4 + x)], own_ref.at[k], sem.at[2 * k]))
        copies.append(pltpu.make_async_copy(a_ref.at[k, rows_of((1 - yl) * 4 + x)], other_ref.at[k], sem.at[2 * k + 1]))
    for cp in copies:
        cp.start()
    for cp in copies:
        cp.wait()


def pick_rows(ids, a):
    shape = jax.ShapeDtypeStruct((4, 128, 256), BF)
    return pl.pallas_call(
        pick_kernel,
        out_shape=[shape, shape],
        in_specs=[pl.BlockSpec(memory_space=pltpu.SMEM), pl.BlockSpec(memory_space=pl.ANY)],
        out_specs=[pl.BlockSpec(memory_space=pltpu.VMEM)] * 2,
        scratch_shapes=[pltpu.SemaphoreType.DMA((8,))],
        compiler_params=pltpu.CompilerParams(vmem_limit_bytes=60 * 2**20),
        cost_estimate=cost(2),
        name="pick_rows",
    )(ids, a)


def rollout_kernel(ids_ref, *refs):
    pieces, (got, turned, a_own, a_other) = refs[:32], refs[32:36]
    outs = refs[36:44]
    w, x, a, b, pre, sem = refs[44:]
    z, c, yl, xx = ids_ref[1], ids_ref[2], ids_ref[3], ids_ref[4]
    copies = []

    def copy(src, dst):
        copies.append(pltpu.make_async_copy(src, dst, sem.at[len(copies)]))

    for k in range(4):
        r = 2 * lax.rem(xx - k + 4, 4)
        copy(got.at[k, 0], x.at[:, pl.ds(pl.multiple_of(r * 256, 256), 256)])
        copy(turned.at[k], x.at[:, pl.ds(pl.multiple_of(r * 256 + 256, 256), 256)])
        copy(a_own.at[k], a.at[r])
        copy(a_other.at[k], a.at[r + 1])
        copy(got.at[k, 2], b.at[r])
        copy(got.at[k, 3], b.at[r + 1])
    for i in range(32):
        d, core, dx = (0, 1, -1, 2)[i // 8], (i // 4) % 2, i % 4
        zz = lax.rem(z - d + 8, 4)
        cc = c if core == 0 else 1 - c
        r = 2 * lax.rem(xx - zz * 2 - cc + 8, 4) + jnp.where(zz // 2 == yl, 0, 1)
        copy(pieces[i], w.at[slice(2 * dx, 2 * dx + 2), pl.ds(pl.multiple_of(r * 256, 256), 256)])
    for cp in copies:
        cp.start()
    for cp in copies:
        cp.wait()

    def step(_, carry):
        cur = x[...]
        dots = jnp.zeros((128, 1), F32)
        for r in range(8):
            block = cur[:, r * 256:(r + 1) * 256].astype(F32)
            dots += jnp.sum(block * a[r].astype(F32), axis=1, keepdims=True)
        gain = SCALE * dots
        for r in range(8):
            pre[:, r * 256:(r + 1) * 256] = jnp.dot(cur, w[r], preferred_element_type=F32)
        for r in range(8):
            cols = slice(r * 256, (r + 1) * 256)
            x[:, cols] = jnp.tanh(pre[:, cols] + gain * b[r].astype(F32)).astype(BF)
        return carry

    lax.fori_loop(0, STEPS, step, 0)
    for r in range(8):
        outs[r][...] = x[:, r * 256:(r + 1) * 256]


def rollout(ids, pieces, members):
    return pl.pallas_call(
        rollout_kernel,
        out_shape=[jax.ShapeDtypeStruct((128, 256), BF)] * 8,
        in_specs=[pl.BlockSpec(memory_space=pltpu.SMEM)] + [pl.BlockSpec(memory_space=pl.ANY)] * 36,
        out_specs=[pl.BlockSpec(memory_space=pltpu.VMEM)] * 8,
        scratch_shapes=[
            pltpu.VMEM((8, 2048, 256), BF),
            pltpu.VMEM((128, 2048), BF),
            pltpu.VMEM((8, 128, 256), BF),
            pltpu.VMEM((8, 128, 256), BF),
            pltpu.VMEM((128, 2048), F32),
            pltpu.SemaphoreType.DMA((56,)),
        ],
        compiler_params=pltpu.CompilerParams(vmem_limit_bytes=60 * 2**20),
        cost_estimate=cost(20),
        name="rollout",
    )(ids, *pieces, *members)


def update_kernel(ids_ref, norm_ref, a_ref, b0, b1, keep_ref, send_ref):
    first = ids_ref[2] == 0
    for k in range(4):
        scaled = (norm_ref[...] * a_ref[k].astype(F32)).astype(BF)
        for h, b in enumerate((b0, b1)):
            d = lax.dot_general(scaled, b[...], (((0,), (0,)), ((), ())), preferred_element_type=F32)
            d = d.reshape(2, 2, 64, 256)
            cols = slice(h * 256, (h + 1) * 256)
            keep_ref[2 * k:2 * k + 2, :, cols] = jnp.where(first, d[:, 0], d[:, 1])
            send_ref[2 * k:2 * k + 2, :, cols] = jnp.where(first, d[:, 1], d[:, 0])


def partial_update(ids, norm, a, b):
    shape = jax.ShapeDtypeStruct((8, 64, 512), F32)
    return pl.pallas_call(
        update_kernel,
        out_shape=[shape, shape],
        in_specs=[pl.BlockSpec(memory_space=pltpu.SMEM)] + [pl.BlockSpec(memory_space=pltpu.VMEM)] * 4,
        out_specs=[pl.BlockSpec(memory_space=pltpu.VMEM)] * 2,
        compiler_params=pltpu.CompilerParams(vmem_limit_bytes=60 * 2**20),
        cost_estimate=cost(10),
        name="partial_update",
    )(ids, norm, a, *b)


def join_kernel(ids_ref, *refs):
    pieces, out_ref = refs[:8], refs[8]
    yl, x = ids_ref[3], ids_ref[4]
    for k, (dy, dx) in enumerate(SHIFTS):
        block = (yl if dy == 0 else 1 - yl) * 4 + lax.rem(x + dx, 4)
        out_ref[rows_of(block), :] = pieces[k][...]


def join_members(ids, pieces):
    return pl.pallas_call(
        join_kernel,
        out_shape=jax.ShapeDtypeStruct((1024, 256), BF),
        in_specs=[pl.BlockSpec(memory_space=pltpu.SMEM)] + [pl.BlockSpec(memory_space=pltpu.VMEM)] * 8,
        out_specs=pl.BlockSpec(memory_space=pltpu.VMEM),
        compiler_params=pltpu.CompilerParams(vmem_limit_bytes=60 * 2**20),
        name="join_members",
    )(ids, *pieces)


def local(states, weight, noise_in, noise_out, fitness):
    yh, z, c = (lax.axis_index(n) for n in POP_AXES)
    yl, x = (lax.axis_index(n) for n in COL_AXES)
    ids = jnp.stack([yh, z, c, yl, x]).astype(jnp.int32)

    with jax.named_scope("swap_b"):
        b = [noise_out, swap(noise_out, "yl")]

    with jax.named_scope("gather_a"):
        a = lax.all_gather(noise_in, "x", axis=0)

    with jax.named_scope("weight_rows"):
        share = lax.dynamic_slice_in_dim(weight, (z % 4) * 512 + c * 256, 256, 0)
        own = [jnp.stack([share, swap(share, "yl")])]
        own += [shift(own[0], "x", dx) for dx in (1, 2, 3)]

    with jax.named_scope("fitness"):
        two = jnp.stack([fitness, swap(fitness, "c")])
        four = jnp.stack([two, swap(two, "yh")])

    with jax.named_scope("members"):
        parts = split_members(ids, states, *b)
        got = lax.all_to_all(after(parts, own[2]), "x", 0, 0)
        turned = swap(got[:, 1], "yl")
        a_own, a_far = pick_rows(ids, a)
        a_other = swap(a_far, "yl")

    with jax.named_scope("weight_ring"):
        up = [shift(v, "z", 1) for v in own]
        down = [shift(v, "z", -1) for v in own]
        far = [shift(up[0], "z", 1), shift(up[1], "z", 1), shift(down[2], "z", -1), shift(down[3], "z", -1)]
        pieces = []
        for part in (own, up, down, far):
            pieces += part + [swap(v, "c") for v in part]

    with jax.named_scope("fitness"):
        four = after(four, own[2])
        everyone = lax.all_to_all(jnp.broadcast_to(four.reshape(1, 32, 128), (8, 32, 128)), "z", 0, 0)
        mean = jnp.sum(everyone) / POP
        var = jnp.sum((everyone - mean) ** 2) / POP
        normed = (fitness - mean) / jnp.sqrt(var + 1e-05)

    with jax.named_scope("update"):
        keep, send = partial_update(ids, normed.reshape(1024, 1), a, b)
        both = after((keep + swap(send, "c")).astype(BF), far[1], far[2], far[3])
        stacked = lax.all_to_all(both, "z", 0, 0)
        total = jnp.sum(stacked.astype(F32), axis=0)
        left, right = total[:, :256], total[:, 256:]
        same = yh == yl
        one = jnp.where(same, left, right)
        two = jnp.where(same, right, left)
        pairs = [(i, j) for i in range(2) for j in range(2)]
        one = lax.ppermute(one, ("yh", "yl"), [(i * 2 + j, j * 2 + i) for i, j in pairs])
        two = lax.ppermute(two, ("yh", "yl"), [(i * 2 + j, j * 2 + (1 - i)) for i, j in pairs])
        update = (one + two) / jnp.sqrt(jnp.float32(POP))

    with jax.named_scope("rollout"):
        done = rollout(ids, pieces, [got, turned, a_own, a_other])
    with jax.named_scope("states_back"):
        back = [done[0]] + [col_shift(done[k], dy, -dx) for k, (dy, dx) in enumerate(SHIFTS) if k > 0]
        final = join_members(ids, back)
    return final, update


def solution(mesh):
    fine = Mesh(mesh.devices.reshape(2, 8, 2, 2, 4), POP_AXES + COL_AXES)
    both = P(POP_AXES, COL_AXES)
    return jax.shard_map(
        local,
        mesh=fine,
        in_specs=(both, P(None, COL_AXES), both, both, P(POP_AXES)),
        out_specs=(both, both),
        check_vma=False,
    )
```

```python
import jax
import jax.numpy as jnp
from jax import lax
from jax.experimental import pallas as pl
from jax.experimental.pallas import tpu as pltpu
from jax.sharding import Mesh, PartitionSpec as P

STEPS = 4
SCALE = 0.02
POP = 32768
POP_AXES = ("yh", "z", "c")
COL_AXES = ("yl", "x")
SHIFTS = [(dy, dx) for dy in range(2) for dx in range(4)]
BF = jnp.bfloat16
F32 = jnp.float32


def col_shift(v, dy, dx):
    perm = []
    for yl in range(2):
        for x in range(4):
            perm.append((yl * 4 + x, (yl ^ dy) * 4 + (x + dx) % 4))
    return lax.ppermute(v, COL_AXES, perm)


def shift(v, axis, d):
    n = 8 if axis == "z" else 4
    return lax.ppermute(v, axis, [(i, (i + d) % n) for i in range(n)])


def over_x(v):
    return lax.all_to_all(v, "x", 0, 0)


def swap(v, axis):
    return lax.ppermute(v, axis, [(0, 1), (1, 0)])


def after(v, *deps):
    return lax.optimization_barrier((v,) + deps)[0]


def rows_of(block):
    return pl.ds(pl.multiple_of(block * 128, 128), 128)


def cost(us):
    return pl.CostEstimate(flops=int(us * 1.15e9), bytes_accessed=0, transcendentals=0)


def split_kernel(ids_ref, s_ref, b_ref, o_ref, out_ref):
    yl = ids_ref[3]
    for k in range(4):
        mine, other = rows_of(yl * 4 + k), rows_of((1 - yl) * 4 + k)
        out_ref[k, 0] = s_ref[mine, :]
        out_ref[k, 1] = s_ref[other, :]
        out_ref[k, 2] = b_ref[mine, :]
        out_ref[k, 3] = o_ref[mine, :]


def split_members(ids, states, b, other):
    return pl.pallas_call(
        split_kernel,
        out_shape=jax.ShapeDtypeStruct((4, 4, 128, 256), BF),
        in_specs=[pl.BlockSpec(memory_space=pltpu.SMEM)] + [pl.BlockSpec(memory_space=pltpu.VMEM)] * 3,
        out_specs=pl.BlockSpec(memory_space=pltpu.VMEM),
        compiler_params=pltpu.CompilerParams(vmem_limit_bytes=60 * 2**20),
        cost_estimate=cost(0.05),
        name="split_members",
    )(ids, states, b, other)


def pick_kernel(ids_ref, a0, a1, a2, lo, hi, own_ref, other_ref, sem):
    yl, x = ids_ref[3], ids_ref[4]
    copies = []
    for dst, block in ((own_ref, yl * 4 + x), (other_ref, (1 - yl) * 4 + x)):
        rows = rows_of(block)
        for k, a in enumerate((a0, a1, a2)):
            copies.append(pltpu.make_async_copy(a.at[rows], dst.at[k], sem.at[len(copies)]))
        for k, a in enumerate((lo, hi)):
            copies.append(pltpu.make_async_copy(a.at[rows], dst.at[3, :, pl.ds(128 * k, 128)], sem.at[len(copies)]))
    for cp in copies:
        cp.start()
    for cp in copies:
        cp.wait()


def pick_rows(ids, a):
    shape = jax.ShapeDtypeStruct((4, 128, 256), BF)
    return pl.pallas_call(
        pick_kernel,
        out_shape=[shape, shape],
        in_specs=[pl.BlockSpec(memory_space=pltpu.SMEM)] + [pl.BlockSpec(memory_space=pl.ANY)] * 5,
        out_specs=[pl.BlockSpec(memory_space=pltpu.VMEM)] * 2,
        scratch_shapes=[pltpu.SemaphoreType.DMA((10,))],
        compiler_params=pltpu.CompilerParams(vmem_limit_bytes=60 * 2**20),
        cost_estimate=cost(0.05),
        name="pick_rows",
    )(ids, *a)


def rollout_kernel(ids_ref, *refs):
    pieces, (got, turned, a_own, a_other) = refs[:16], refs[16:20]
    outs = refs[20:28]
    w, x, a, b, pre, sem = refs[28:]
    z, c, yl, xx = ids_ref[1], ids_ref[2], ids_ref[3], ids_ref[4]
    copies = []

    def copy(src, dst):
        copies.append(pltpu.make_async_copy(src, dst, sem.at[len(copies)]))

    for k in range(4):
        r = (0, 1, 3, 2)[k]
        copy(a_own.at[k], a.at[r])
        copy(a_other.at[k], a.at[r + 4])
        r = lax.rem(xx - k + 4, 4)
        copy(got.at[k, 0], x.at[:, pl.ds(pl.multiple_of(r * 256, 256), 256)])
        copy(turned.at[k], x.at[:, pl.ds(pl.multiple_of(r * 256 + 1024, 256), 256)])
        copy(got.at[k, 2], b.at[r])
        copy(got.at[k, 3], b.at[r + 4])
    for part in range(2):
        for i in range(part, 16, 2):
            d, core = (0, 1, -1, 2)[i // 4], (i // 2) % 2
            zz = lax.rem(z - d + 8, 4)
            cc = c if core == 0 else 1 - c
            r = jnp.where(zz // 2 == yl, 0, 4) + lax.rem(xx - zz * 2 - cc + 8, 4)
            copy(pieces[i], w.at[slice(4 * part, 4 * part + 4), pl.ds(pl.multiple_of(r * 256, 256), 256)])
    for cp in copies:
        cp.start()

    def multiply(cur, blocks):
        for r in blocks:
            pre[:, r * 256:(r + 1) * 256] = jnp.dot(cur, w[r], preferred_element_type=F32)

    def gain_of(cur):
        dots = jnp.zeros((128, 1), F32)
        for r in range(8):
            block = cur[:, r * 256:(r + 1) * 256].astype(F32)
            dots += jnp.sum(block * a[r].astype(F32), axis=1, keepdims=True)
        return SCALE * dots

    def finish(gain):
        for r in range(8):
            cols = slice(r * 256, (r + 1) * 256)
            x[:, cols] = jnp.tanh(pre[:, cols] + gain * b[r].astype(F32)).astype(BF)

    for cp in copies[:24]:
        cp.wait()
    cur = x[...]
    gain = gain_of(cur)
    for cp in copies[24:32]:
        cp.wait()
    multiply(cur, range(4))
    for cp in copies[32:]:
        cp.wait()
    multiply(cur, range(4, 8))
    finish(gain)

    def step(_, carry):
        cur = x[...]
        gain = gain_of(cur)
        multiply(cur, range(8))
        finish(gain)
        return carry

    lax.fori_loop(1, STEPS, step, 0)
    for k in range(8):
        outs[k][...] = x[:, k * 256:(k + 1) * 256]


def rollout(ids, pieces, members):
    return pl.pallas_call(
        rollout_kernel,
        out_shape=[jax.ShapeDtypeStruct((128, 256), BF)] * 8,
        in_specs=[pl.BlockSpec(memory_space=pltpu.SMEM)] + [pl.BlockSpec(memory_space=pl.ANY)] * 20,
        out_specs=[pl.BlockSpec(memory_space=pltpu.VMEM)] * 8,
        scratch_shapes=[
            pltpu.VMEM((8, 2048, 256), BF),
            pltpu.VMEM((128, 2048), BF),
            pltpu.VMEM((8, 128, 256), BF),
            pltpu.VMEM((8, 128, 256), BF),
            pltpu.VMEM((128, 2048), F32),
            pltpu.SemaphoreType.DMA((40,)),
        ],
        compiler_params=pltpu.CompilerParams(vmem_limit_bytes=60 * 2**20),
        cost_estimate=cost(0.05),
        name="rollout",
    )(ids, *pieces, *members)


def update_kernel(ids_ref, norm_ref, a0, a1, a2, lo, hi, b0, b1, keep_ref, send_ref):
    first = ids_ref[2] == 0
    x = ids_ref[4]
    where = [lax.rem(x + d, 4) for d in (0, 3, 1, 2)]
    for k, a in enumerate((a0, a1, a2, lo, hi)):
        scaled = (norm_ref[...] * a[...].astype(F32)).astype(BF)
        n = scaled.shape[1] // 128
        row = 2 * where[min(k, 3)] + (1 if k == 4 else 0)
        for h, b in enumerate((b0, b1)):
            d = lax.dot_general(scaled, b[...], (((0,), (0,)), ((), ())), preferred_element_type=F32)
            d = d.reshape(n, 2, 64, 256).astype(BF)
            cols = slice(h * 256, (h + 1) * 256)
            keep_ref[pl.ds(row, n), :, cols] = jnp.where(first, d[:, 0], d[:, 1])
            send_ref[pl.ds(row, n), :, cols] = jnp.where(first, d[:, 1], d[:, 0])


def partial_update(ids, norm, a, b):
    shape = jax.ShapeDtypeStruct((8, 64, 512), BF)
    return pl.pallas_call(
        update_kernel,
        out_shape=[shape, shape],
        in_specs=[pl.BlockSpec(memory_space=pltpu.SMEM)] + [pl.BlockSpec(memory_space=pltpu.VMEM)] * 8,
        out_specs=[pl.BlockSpec(memory_space=pltpu.VMEM)] * 2,
        compiler_params=pltpu.CompilerParams(vmem_limit_bytes=60 * 2**20),
        cost_estimate=cost(0.05),
        name="partial_update",
    )(ids, norm, *a, *b)


def join_kernel(ids_ref, *refs):
    pieces, out_ref = refs[:8], refs[8]
    yl, x = ids_ref[3], ids_ref[4]
    for k, (dy, dx) in enumerate(SHIFTS):
        block = (yl if dy == 0 else 1 - yl) * 4 + lax.rem(x + dx, 4)
        out_ref[rows_of(block), :] = pieces[k][...]


def join_members(ids, pieces):
    return pl.pallas_call(
        join_kernel,
        out_shape=jax.ShapeDtypeStruct((1024, 256), BF),
        in_specs=[pl.BlockSpec(memory_space=pltpu.SMEM)] + [pl.BlockSpec(memory_space=pltpu.VMEM)] * 8,
        out_specs=pl.BlockSpec(memory_space=pltpu.VMEM),
        compiler_params=pltpu.CompilerParams(vmem_limit_bytes=60 * 2**20),
        name="join_members",
    )(ids, *pieces)


def local(states, weight, noise_in, noise_out, fitness):
    yh, z, c = (lax.axis_index(n) for n in POP_AXES)
    yl, x = (lax.axis_index(n) for n in COL_AXES)
    ids = jnp.stack([yh, z, c, yl, x]).astype(jnp.int32)

    with jax.named_scope("weight_rows"):
        share = lax.dynamic_slice_in_dim(weight, (z % 4) * 512 + c * 256, 256, 0)
        partner = swap(share, "yl")
        own = [jnp.stack([share] + [shift(share, "x", dx) for dx in (1, 2, 3)])]
        partner = after(partner, own[0])
        own.append(jnp.stack([partner] + [shift(partner, "x", dx) for dx in (1, 2, 3)]))

    with jax.named_scope("fitness"):
        two = jnp.stack([fitness, swap(after(fitness, share), "c")])
        four = jnp.stack([two, swap(two, "yh")])

    with jax.named_scope("round_1"):
        first, a_in, four = lax.optimization_barrier((own[0], noise_in, four))
        up, down = [shift(first, "z", 1)], [shift(first, "z", -1)]
        left, right = shift(a_in, "x", 1), shift(a_in, "x", -1)
        b = [noise_out, swap(noise_out, "yl")]
        four = after(four, own[1])
        everyone = lax.all_to_all(jnp.broadcast_to(four.reshape(1, 32, 128), (8, 32, 128)), "z", 0, 0)
        parts = split_members(ids, states, *b)

    with jax.named_scope("round_2"):
        second, left, right, parts = lax.optimization_barrier(
            (own[1], left, right, parts, up[0], down[0], everyone)
        )[:4]
        up.append(shift(second, "z", 1))
        down.append(shift(second, "z", -1))
        a = [noise_in, left, right, shift(left[:, :128], "x", 1), shift(right[:, 128:], "x", -1)]
        got = over_x(parts)
        others = [swap(v, "c") for v in (*own, up[0], down[0])]

    with jax.named_scope("round_3"):
        fore, back, turn, *a = lax.optimization_barrier((up[0], down[1], got[:, 1], *a, up[1]))[:8]
        far = [shift(fore, "z", 1), shift(back, "z", -1)]
        near = [swap(v, "c") for v in (up[1], down[1])]
        turned = swap(turn, "yl")
        a_own, a_far = pick_rows(ids, lax.optimization_barrier((*a, *near))[:5])
        a_other = swap(a_far, "yl")

    with jax.named_scope("weight"):
        last = lax.optimization_barrier((*far, *near, *others, a_other, turned))[:2]
        pieces = own + others[:2] + up + [others[2], near[0]] + down + [others[3], near[1]]
        pieces += far + [swap(v, "c") for v in last]

    with jax.named_scope("fitness"):
        mean = jnp.sum(everyone) / POP
        var = jnp.sum((everyone - mean) ** 2) / POP
        normed = (fitness - mean) / jnp.sqrt(var + 1e-05)
        normed = after(normed, a_far)

    with jax.named_scope("update"):
        keep, send = partial_update(ids, normed.reshape(1024, 1), a, b)
        both = after((keep.astype(F32) + swap(send, "c").astype(F32)).astype(BF), *far)
        stacked = lax.all_to_all(both, "z", 0, 0)
        total = jnp.sum(stacked.astype(F32), axis=0)
        left, right = total[:, :256], total[:, 256:]
        same = yh == yl
        one = jnp.where(same, left, right)
        two = jnp.where(same, right, left)
        pairs = [(i, j) for i in range(2) for j in range(2)]
        one = lax.ppermute(one, ("yh", "yl"), [(i * 2 + j, j * 2 + i) for i, j in pairs])
        two = lax.ppermute(two, ("yh", "yl"), [(i * 2 + j, j * 2 + (1 - i)) for i, j in pairs])
        update = (one + two) / jnp.sqrt(jnp.float32(POP))

    with jax.named_scope("rollout"):
        done = rollout(ids, pieces, [got, turned, a_own, a_other])
    with jax.named_scope("states_back"):
        back = [done[0]] + [col_shift(done[k], dy, -dx) for k, (dy, dx) in enumerate(SHIFTS) if k > 0]
        final = join_members(ids, back)
    return final, update


def solution(mesh):
    fine = Mesh(mesh.devices.reshape(2, 8, 2, 2, 4), POP_AXES + COL_AXES)
    both = P(POP_AXES, COL_AXES)
    return jax.shard_map(
        local,
        mesh=fine,
        in_specs=(both, P(None, COL_AXES), both, both, P(POP_AXES)),
        out_specs=(both, both),
        check_vma=False,
    )
```

```python
import jax
import jax.numpy as jnp
from jax import lax
from jax.experimental import pallas as pl
from jax.experimental.pallas import tpu as pltpu
from jax.sharding import Mesh, PartitionSpec as P

STEPS = 4
SCALE = 0.02
POP = 32768
POP_AXES = ("yh", "z", "c")
COL_AXES = ("yl", "x")
SHIFTS = [(dy, dx) for dy in range(2) for dx in range(4)]
BF = jnp.bfloat16
F32 = jnp.float32


def col_shift(v, dy, dx):
    perm = []
    for yl in range(2):
        for x in range(4):
            perm.append((yl * 4 + x, (yl ^ dy) * 4 + (x + dx) % 4))
    return lax.ppermute(v, COL_AXES, perm)


def shift(v, axis, d):
    n = 8 if axis == "z" else 4
    return lax.ppermute(v, axis, [(i, (i + d) % n) for i in range(n)])


def over_x(v):
    return lax.all_to_all(v, "x", 0, 0)


def swap(v, axis):
    return lax.ppermute(v, axis, [(0, 1), (1, 0)])


def after(v, *deps):
    return lax.optimization_barrier((v,) + deps)[0]


def rows_of(block):
    return pl.ds(pl.multiple_of(block * 128, 128), 128)


def cost(us):
    return pl.CostEstimate(flops=int(us * 1.15e9), bytes_accessed=0, transcendentals=0)


def split_kernel(ids_ref, s_ref, b_ref, o_ref, out_ref):
    yl = ids_ref[3]
    for k in range(4):
        mine, other = rows_of(yl * 4 + k), rows_of((1 - yl) * 4 + k)
        out_ref[k, 0] = s_ref[mine, :]
        out_ref[k, 1] = s_ref[other, :]
        out_ref[k, 2] = b_ref[mine, :]
        out_ref[k, 3] = o_ref[mine, :]


def split_members(ids, states, b, other):
    return pl.pallas_call(
        split_kernel,
        out_shape=jax.ShapeDtypeStruct((4, 4, 128, 256), BF),
        in_specs=[pl.BlockSpec(memory_space=pltpu.SMEM)] + [pl.BlockSpec(memory_space=pltpu.VMEM)] * 3,
        out_specs=pl.BlockSpec(memory_space=pltpu.VMEM),
        compiler_params=pltpu.CompilerParams(vmem_limit_bytes=60 * 2**20),
        cost_estimate=cost(0.05),
        name="split_members",
    )(ids, states, b, other)


def pick_kernel(ids_ref, a0, a1, a2, lo, hi, own_ref, other_ref, sem):
    yl, x = ids_ref[3], ids_ref[4]
    copies = []
    for dst, block in ((own_ref, yl * 4 + x), (other_ref, (1 - yl) * 4 + x)):
        rows = rows_of(block)
        for k, a in enumerate((a0, a1, a2)):
            copies.append(pltpu.make_async_copy(a.at[rows], dst.at[k], sem.at[len(copies)]))
        for k, a in enumerate((lo, hi)):
            copies.append(pltpu.make_async_copy(a.at[rows], dst.at[3, :, pl.ds(128 * k, 128)], sem.at[len(copies)]))
    for cp in copies:
        cp.start()
    for cp in copies:
        cp.wait()


def pick_rows(ids, a):
    shape = jax.ShapeDtypeStruct((4, 128, 256), BF)
    return pl.pallas_call(
        pick_kernel,
        out_shape=[shape, shape],
        in_specs=[pl.BlockSpec(memory_space=pltpu.SMEM)] + [pl.BlockSpec(memory_space=pl.ANY)] * 5,
        out_specs=[pl.BlockSpec(memory_space=pltpu.VMEM)] * 2,
        scratch_shapes=[pltpu.SemaphoreType.DMA((10,))],
        compiler_params=pltpu.CompilerParams(vmem_limit_bytes=60 * 2**20),
        cost_estimate=cost(0.05),
        name="pick_rows",
    )(ids, *a)


def rollout_kernel(ids_ref, *refs):
    pieces, (got, turned, a_own, a_other) = refs[:20], refs[20:24]
    outs = refs[24:32]
    w, x, a, b, pre, sem = refs[32:]
    z, c, yl, xx = ids_ref[1], ids_ref[2], ids_ref[3], ids_ref[4]
    copies = []

    def copy(src, dst):
        copies.append(pltpu.make_async_copy(src, dst, sem.at[len(copies)]))

    for k in range(4):
        r = (0, 1, 3, 2)[k]
        copy(a_own.at[k], a.at[r])
        copy(a_other.at[k], a.at[r + 4])
        r = lax.rem(xx - k + 4, 4)
        copy(got.at[k, 0], x.at[:, pl.ds(pl.multiple_of(r * 256, 256), 256)])
        copy(turned.at[k], x.at[:, pl.ds(pl.multiple_of(r * 256 + 1024, 256), 256)])
        copy(got.at[k, 2], b.at[r])
        copy(got.at[k, 3], b.at[r + 4])
    def rows_at(d, core):
        zz = lax.rem(z - d + 8, 4)
        cc = c if core == 0 else 1 - c
        r = jnp.where(zz // 2 == yl, 0, 4) + lax.rem(xx - zz * 2 - cc + 8, 4)
        return pl.ds(pl.multiple_of(r * 256, 256), 256)

    for part in range(2):
        cols = (slice(0, 5), slice(5, 8))[part]
        for i in range(part, 12, 2):
            copy(pieces[i], w.at[cols, rows_at((0, 1, -1)[i // 4], (i // 2) % 2)])
        for core in range(2):
            first, second = pieces[12 + 4 * core + part], pieces[14 + 4 * core + part]
            rows = rows_at(2, core)
            if part == 0:
                copy(first, w.at[slice(0, 2), rows])
                copy(second, w.at[slice(2, 4), rows])
            else:
                copy(first, w.at[slice(5, 7), rows])
                copy(second.at[0], w.at[4, rows])
                copy(second.at[1], w.at[7, rows])
    for cp in copies:
        cp.start()

    def multiply(cur, blocks):
        for r in blocks:
            pre[:, r * 256:(r + 1) * 256] = jnp.dot(cur, w[r], preferred_element_type=F32)

    def gain_of(cur):
        dots = jnp.zeros((128, 1), F32)
        for r in range(8):
            block = cur[:, r * 256:(r + 1) * 256].astype(F32)
            dots += jnp.sum(block * a[r].astype(F32), axis=1, keepdims=True)
        return SCALE * dots

    def finish(gain):
        for r in range(8):
            cols = slice(r * 256, (r + 1) * 256)
            x[:, cols] = jnp.tanh(pre[:, cols] + gain * b[r].astype(F32)).astype(BF)

    for cp in copies[:24]:
        cp.wait()
    cur = x[...]
    gain = gain_of(cur)
    for cp in copies[24:34]:
        cp.wait()
    multiply(cur, range(4))
    for cp in copies[34:]:
        cp.wait()
    multiply(cur, range(4, 8))
    finish(gain)

    def step(_, carry):
        cur = x[...]
        gain = gain_of(cur)
        multiply(cur, range(8))
        finish(gain)
        return carry

    lax.fori_loop(1, STEPS, step, 0)
    for k in range(8):
        outs[k][...] = x[:, k * 256:(k + 1) * 256]


def rollout(ids, pieces, members):
    return pl.pallas_call(
        rollout_kernel,
        out_shape=[jax.ShapeDtypeStruct((128, 256), BF)] * 8,
        in_specs=[pl.BlockSpec(memory_space=pltpu.SMEM)] + [pl.BlockSpec(memory_space=pl.ANY)] * 24,
        out_specs=[pl.BlockSpec(memory_space=pltpu.VMEM)] * 8,
        scratch_shapes=[
            pltpu.VMEM((8, 2048, 256), BF),
            pltpu.VMEM((128, 2048), BF),
            pltpu.VMEM((8, 128, 256), BF),
            pltpu.VMEM((8, 128, 256), BF),
            pltpu.VMEM((128, 2048), F32),
            pltpu.SemaphoreType.DMA((46,)),
        ],
        compiler_params=pltpu.CompilerParams(vmem_limit_bytes=60 * 2**20),
        cost_estimate=cost(0.05),
        name="rollout",
    )(ids, *pieces, *members)


def update_kernel(ids_ref, norm_ref, a0, a1, a2, lo, hi, b0, b1, keep_ref, send_ref):
    first = ids_ref[2] == 0
    x = ids_ref[4]
    where = [lax.rem(x + d, 4) for d in (0, 3, 1, 2)]
    for k, a in enumerate((a0, a1, a2, lo, hi)):
        scaled = (norm_ref[...] * a[...].astype(F32)).astype(BF)
        n = scaled.shape[1] // 128
        row = 2 * where[min(k, 3)] + (1 if k == 4 else 0)
        for h, b in enumerate((b0, b1)):
            d = lax.dot_general(scaled, b[...], (((0,), (0,)), ((), ())), preferred_element_type=F32)
            d = d.reshape(n, 2, 64, 256).astype(BF)
            cols = slice(h * 256, (h + 1) * 256)
            keep_ref[pl.ds(row, n), :, cols] = jnp.where(first, d[:, 0], d[:, 1])
            send_ref[pl.ds(row, n), :, cols] = jnp.where(first, d[:, 1], d[:, 0])


def partial_update(ids, norm, a, b):
    shape = jax.ShapeDtypeStruct((8, 64, 512), BF)
    return pl.pallas_call(
        update_kernel,
        out_shape=[shape, shape],
        in_specs=[pl.BlockSpec(memory_space=pltpu.SMEM)] + [pl.BlockSpec(memory_space=pltpu.VMEM)] * 8,
        out_specs=[pl.BlockSpec(memory_space=pltpu.VMEM)] * 2,
        compiler_params=pltpu.CompilerParams(vmem_limit_bytes=60 * 2**20),
        cost_estimate=cost(0.05),
        name="partial_update",
    )(ids, norm, *a, *b)


def join_kernel(ids_ref, *refs):
    pieces, out_ref = refs[:8], refs[8]
    yl, x = ids_ref[3], ids_ref[4]
    for k, (dy, dx) in enumerate(SHIFTS):
        block = (yl if dy == 0 else 1 - yl) * 4 + lax.rem(x + dx, 4)
        out_ref[rows_of(block), :] = pieces[k][...]


def join_members(ids, pieces):
    return pl.pallas_call(
        join_kernel,
        out_shape=jax.ShapeDtypeStruct((1024, 256), BF),
        in_specs=[pl.BlockSpec(memory_space=pltpu.SMEM)] + [pl.BlockSpec(memory_space=pltpu.VMEM)] * 8,
        out_specs=pl.BlockSpec(memory_space=pltpu.VMEM),
        compiler_params=pltpu.CompilerParams(vmem_limit_bytes=60 * 2**20),
        name="join_members",
    )(ids, *pieces)


def local(states, weight, noise_in, noise_out, fitness):
    yh, z, c = (lax.axis_index(n) for n in POP_AXES)
    yl, x = (lax.axis_index(n) for n in COL_AXES)
    ids = jnp.stack([yh, z, c, yl, x]).astype(jnp.int32)

    with jax.named_scope("weight_rows"):
        share = lax.dynamic_slice_in_dim(weight, (z % 4) * 512 + c * 256, 256, 0)
        partner = swap(share, "yl")
        moved = [shift(share, "x", dx) for dx in (1, 2, 3)]
        two = jnp.stack([fitness, swap(after(fitness, share), "c")])
        own = [jnp.stack([share] + moved + [partner])]
        four = jnp.stack([two, swap(two, "yh")])

    with jax.named_scope("round_1"):
        up, down = [shift(own[0], "z", 1)], [shift(own[0], "z", -1)]
        partner, four, a_in = lax.optimization_barrier((partner, four, noise_in, own[0]))[:3]
        own.append(jnp.stack([shift(partner, "x", dx) for dx in (1, 2, 3)]))
        left, right = shift(a_in, "x", 1), shift(a_in, "x", -1)
        b = [noise_out, swap(noise_out, "yl")]
        everyone = lax.all_to_all(jnp.broadcast_to(four.reshape(1, 32, 128), (8, 32, 128)), "z", 0, 0)
        parts = split_members(ids, states, *b)

    with jax.named_scope("round_2"):
        second, parts, left, right = lax.optimization_barrier(
            (own[1], parts, left, right, up[0], down[0], everyone)
        )[:4]
        up.append(shift(second, "z", 1))
        down.append(shift(second, "z", -1))
        a = [noise_in, left, right, shift(left[:, :128], "x", 1), shift(right[:, 128:], "x", -1)]
        got = over_x(parts)
        others = [swap(v, "c") for v in (*own, up[0], down[0])]

    with jax.named_scope("round_3"):
        fore, back, turn, *a = lax.optimization_barrier((up[0], down[1], got[:, 1], *a, up[1]))[:8]
        far = [shift(fore[:2], "z", 1), shift(back[:2], "z", -1)]
        fore, back = fore[2:4], jnp.concatenate([down[0][4:], back[2:]])
        near = [swap(v, "c") for v in (up[1], down[1])]
        turned = swap(turn, "yl")
        a_own, a_far = pick_rows(ids, a)
        a_other = swap(a_far, "yl")
        mean = jnp.sum(everyone) / POP
        var = jnp.sum((everyone - mean) ** 2) / POP
        normed = (fitness - mean) / jnp.sqrt(var + 1e-05)
        keep, send = partial_update(ids, after(normed, a_far).reshape(1024, 1), a, b)

    with jax.named_scope("round_4"):
        fore, back, send = lax.optimization_barrier((fore, back, send, *far, turned, a_other, keep))[:3]
        far += [shift(fore, "z", 1), shift(back, "z", -1)]
        crossed = [swap(v, "c") for v in far[:2]]

    with jax.named_scope("weight"):
        last = lax.optimization_barrier((*far[2:], *near, *others, *crossed))[:2]
        crossed += [swap(v, "c") for v in last]
        pieces = own + others[:2] + up + [others[2], near[0]] + down + [others[3], near[1]]
        pieces += far + crossed

    with jax.named_scope("update"):
        both = after((keep.astype(F32) + swap(send, "c").astype(F32)).astype(BF), *far[2:])
        stacked = lax.all_to_all(both, "z", 0, 0)
        total = jnp.sum(stacked.astype(F32), axis=0)
        left, right = total[:, :256], total[:, 256:]
        same = yh == yl
        one = jnp.where(same, left, right)
        two = jnp.where(same, right, left)
        pairs = [(i, j) for i in range(2) for j in range(2)]
        one = lax.ppermute(one, ("yh", "yl"), [(i * 2 + j, j * 2 + i) for i, j in pairs])
        two = lax.ppermute(two, ("yh", "yl"), [(i * 2 + j, j * 2 + (1 - i)) for i, j in pairs])
        update = (one + two) / jnp.sqrt(jnp.float32(POP))

    with jax.named_scope("rollout"):
        done = rollout(ids, pieces, [got, turned, a_own, a_other])
    with jax.named_scope("states_back"):
        back = [done[0]] + [col_shift(done[k], dy, -dx) for k, (dy, dx) in enumerate(SHIFTS) if k > 0]
        final = join_members(ids, back)
    return final, update


def solution(mesh):
    fine = Mesh(mesh.devices.reshape(2, 8, 2, 2, 4), POP_AXES + COL_AXES)
    both = P(POP_AXES, COL_AXES)
    return jax.shard_map(
        local,
        mesh=fine,
        in_specs=(both, P(None, COL_AXES), both, both, P(POP_AXES)),
        out_specs=(both, both),
        check_vma=False,
    )
```

```python
import jax
import jax.numpy as jnp
from jax import lax
from jax.experimental import pallas as pl
from jax.experimental.pallas import tpu as pltpu
from jax.sharding import Mesh, PartitionSpec as P

STEPS = 4
SCALE = 0.02
POP = 32768
POP_AXES = ("yh", "z", "c")
COL_AXES = ("yl", "x")
SHIFTS = [(dy, dx) for dy in range(2) for dx in range(4)]
BF = jnp.bfloat16
F32 = jnp.float32


def col_shift(v, dy, dx):
    perm = []
    for yl in range(2):
        for x in range(4):
            perm.append((yl * 4 + x, (yl ^ dy) * 4 + (x + dx) % 4))
    return lax.ppermute(v, COL_AXES, perm)


def shift(v, axis, d):
    n = 8 if axis == "z" else 4
    return lax.ppermute(v, axis, [(i, (i + d) % n) for i in range(n)])


def over_x(v):
    return lax.all_to_all(v, "x", 0, 0)


def swap(v, axis):
    return lax.ppermute(v, axis, [(0, 1), (1, 0)])


def after(v, *deps):
    return lax.optimization_barrier((v,) + deps)[0]


def rows_of(block):
    return pl.ds(pl.multiple_of(block * 128, 128), 128)


def cost(us):
    return pl.CostEstimate(flops=int(us * 1.15e9), bytes_accessed=0, transcendentals=0)


def split_kernel(ids_ref, s_ref, a_ref, b_ref, o_ref, out_ref):
    yl = ids_ref[3]
    for k in range(4):
        mine, other = rows_of(yl * 4 + k), rows_of((1 - yl) * 4 + k)
        for n, (src, rows) in enumerate(
            ((s_ref, mine), (a_ref, mine), (b_ref, mine), (o_ref, mine), (s_ref, other), (a_ref, other))
        ):
            out_ref[k, n] = src[rows, :]


def split_members(ids, states, a, b, other):
    return pl.pallas_call(
        split_kernel,
        out_shape=jax.ShapeDtypeStruct((4, 6, 128, 256), BF),
        in_specs=[pl.BlockSpec(memory_space=pltpu.SMEM)] + [pl.BlockSpec(memory_space=pltpu.VMEM)] * 4,
        out_specs=pl.BlockSpec(memory_space=pltpu.VMEM),
        compiler_params=pltpu.CompilerParams(vmem_limit_bytes=60 * 2**20),
        cost_estimate=cost(0.05),
        name="split_members",
    )(ids, states, a, b, other)


def rollout_kernel(ids_ref, *refs):
    pieces, (got, turned) = refs[:16], refs[16:18]
    outs = refs[18:26]
    w, x, a, b, pre, sem = refs[26:]
    z, c, yl, xx = ids_ref[1], ids_ref[2], ids_ref[3], ids_ref[4]
    copies = []

    def copy(src, dst):
        copies.append(pltpu.make_async_copy(src, dst, sem.at[len(copies)]))

    for k in range(4):
        r = lax.rem(xx - k + 4, 4)
        copy(got.at[k, 0], x.at[:, pl.ds(pl.multiple_of(r * 256, 256), 256)])
        copy(turned.at[k, 0], x.at[:, pl.ds(pl.multiple_of(r * 256 + 1024, 256), 256)])
        copy(got.at[k, 1], a.at[r])
        copy(turned.at[k, 1], a.at[r + 4])
        copy(got.at[k, 2], b.at[r])
        copy(got.at[k, 3], b.at[r + 4])
    for part in range(2):
        for i in range(part, 16, 2):
            d, core = (0, 1, -1, 2)[i // 4], (i // 2) % 2
            zz = lax.rem(z - d + 8, 4)
            cc = c if core == 0 else 1 - c
            r = jnp.where(zz // 2 == yl, 0, 4) + lax.rem(xx - zz * 2 - cc + 8, 4)
            copy(pieces[i], w.at[slice(4 * part, 4 * part + 4), pl.ds(pl.multiple_of(r * 256, 256), 256)])
    for cp in copies:
        cp.start()

    def multiply(cur, blocks):
        for r in blocks:
            pre[:, r * 256:(r + 1) * 256] = jnp.dot(cur, w[r], preferred_element_type=F32)

    def gain_of(cur):
        dots = jnp.zeros((128, 1), F32)
        for r in range(8):
            block = cur[:, r * 256:(r + 1) * 256].astype(F32)
            dots += jnp.sum(block * a[r].astype(F32), axis=1, keepdims=True)
        return SCALE * dots

    def finish(gain):
        for r in range(8):
            cols = slice(r * 256, (r + 1) * 256)
            x[:, cols] = jnp.tanh(pre[:, cols] + gain * b[r].astype(F32)).astype(BF)

    for cp in copies[:24]:
        cp.wait()
    cur = x[...]
    gain = gain_of(cur)
    for cp in copies[24:32]:
        cp.wait()
    multiply(cur, range(4))
    for cp in copies[32:]:
        cp.wait()
    multiply(cur, range(4, 8))
    finish(gain)

    def step(_, carry):
        cur = x[...]
        gain = gain_of(cur)
        multiply(cur, range(8))
        finish(gain)
        return carry

    lax.fori_loop(1, STEPS, step, 0)
    for k in range(8):
        outs[k][...] = x[:, k * 256:(k + 1) * 256]


def rollout(ids, pieces, members):
    return pl.pallas_call(
        rollout_kernel,
        out_shape=[jax.ShapeDtypeStruct((128, 256), BF)] * 8,
        in_specs=[pl.BlockSpec(memory_space=pltpu.SMEM)] + [pl.BlockSpec(memory_space=pl.ANY)] * 18,
        out_specs=[pl.BlockSpec(memory_space=pltpu.VMEM)] * 8,
        scratch_shapes=[
            pltpu.VMEM((8, 2048, 256), BF),
            pltpu.VMEM((128, 2048), BF),
            pltpu.VMEM((8, 128, 256), BF),
            pltpu.VMEM((8, 128, 256), BF),
            pltpu.VMEM((128, 2048), F32),
            pltpu.SemaphoreType.DMA((40,)),
        ],
        compiler_params=pltpu.CompilerParams(vmem_limit_bytes=60 * 2**20),
        cost_estimate=cost(0.05),
        name="rollout",
    )(ids, *pieces, *members)


def update_kernel(ids_ref, all_ref, fit_ref, a0, a1, a2, lo, hi, b0, b1, keep_ref, send_ref):
    first = ids_ref[2] == 0
    x = ids_ref[4]
    where = [lax.rem(x + d, 4) for d in (0, 3, 1, 2)]
    mean = jnp.sum(all_ref[...], keepdims=True).reshape(1, 1) / POP
    var = jnp.sum((all_ref[...] - mean) ** 2, keepdims=True).reshape(1, 1) / POP
    norm = (fit_ref[...] - mean) / jnp.sqrt(var + 1e-05)
    for k, a in enumerate((a0, a1, a2, lo, hi)):
        scaled = (norm * a[...].astype(F32)).astype(BF)
        n = scaled.shape[1] // 128
        row = 2 * where[min(k, 3)] + (1 if k == 4 else 0)
        for h, b in enumerate((b0, b1)):
            d = lax.dot_general(scaled, b[...], (((0,), (0,)), ((), ())), preferred_element_type=F32)
            d = d.reshape(n, 2, 64, 256).astype(BF)
            cols = slice(h * 256, (h + 1) * 256)
            keep_ref[pl.ds(row, n), :, cols] = jnp.where(first, d[:, 0], d[:, 1])
            send_ref[pl.ds(row, n), :, cols] = jnp.where(first, d[:, 1], d[:, 0])


def partial_update(ids, everyone, fitness, a, b):
    shape = jax.ShapeDtypeStruct((8, 64, 512), BF)
    return pl.pallas_call(
        update_kernel,
        out_shape=[shape, shape],
        in_specs=[pl.BlockSpec(memory_space=pltpu.SMEM)] + [pl.BlockSpec(memory_space=pltpu.VMEM)] * 9,
        out_specs=[pl.BlockSpec(memory_space=pltpu.VMEM)] * 2,
        compiler_params=pltpu.CompilerParams(vmem_limit_bytes=60 * 2**20),
        cost_estimate=cost(0.05),
        name="partial_update",
    )(ids, everyone, fitness, *a, *b)


def join_kernel(ids_ref, *refs):
    pieces, out_ref = refs[:8], refs[8]
    yl, x = ids_ref[3], ids_ref[4]
    for k, (dy, dx) in enumerate(SHIFTS):
        block = (yl if dy == 0 else 1 - yl) * 4 + lax.rem(x + dx, 4)
        out_ref[rows_of(block), :] = pieces[k][...]


def join_members(ids, pieces):
    return pl.pallas_call(
        join_kernel,
        out_shape=jax.ShapeDtypeStruct((1024, 256), BF),
        in_specs=[pl.BlockSpec(memory_space=pltpu.SMEM)] + [pl.BlockSpec(memory_space=pltpu.VMEM)] * 8,
        out_specs=pl.BlockSpec(memory_space=pltpu.VMEM),
        compiler_params=pltpu.CompilerParams(vmem_limit_bytes=60 * 2**20),
        name="join_members",
    )(ids, *pieces)


def local(states, weight, noise_in, noise_out, fitness):
    yh, z, c = (lax.axis_index(n) for n in POP_AXES)
    yl, x = (lax.axis_index(n) for n in COL_AXES)
    ids = jnp.stack([yh, z, c, yl, x]).astype(jnp.int32)

    with jax.named_scope("fitness"):
        everyone = lax.all_to_all(jnp.broadcast_to(fitness.reshape(1, 8, 128), (32, 8, 128)), POP_AXES, 0, 0)

    with jax.named_scope("weight_rows"):
        share = lax.dynamic_slice_in_dim(weight, (z % 4) * 512 + c * 256, 256, 0)
        own = [jnp.stack([share] + [shift(share, "x", dx) for dx in (1, 2, 3)])]
        b = [noise_out, swap(noise_out, "yl")]

    with jax.named_scope("round_1"):
        first, a_in = lax.optimization_barrier((own[0], noise_in, everyone))[:2]
        own.append(swap(first, "yl"))
        up, down = [shift(first, "z", 1)], [shift(first, "z", -1)]
        left, right = shift(a_in, "x", 1), shift(a_in, "x", -1)
        parts = split_members(ids, states, noise_in, *b)

    with jax.named_scope("round_2"):
        others = [swap(v, "c") for v in (*own, up[0], down[0])]
        second = after(own[1], *others)
        up.append(shift(second, "z", 1))
        down.append(shift(second, "z", -1))
        got = over_x(after(parts, first))

    with jax.named_scope("round_3"):
        fore, back, turn = lax.optimization_barrier((up[0], down[1], got[:, 4:], up[1]))[:3]
        left, right = lax.optimization_barrier((left, right, up[1], down[1]))[:2]
        far = [shift(fore, "z", 1), shift(back, "z", -1)]
        turned = swap(turn, "yl")
        a = [noise_in, left, right, shift(left[:, :128], "x", 1), shift(right[:, 128:], "x", -1)]
        near = [swap(v, "c") for v in (up[1], down[1])]
        keep, send = partial_update(ids, everyone, fitness.reshape(1024, 1), a, b)

    with jax.named_scope("weight"):
        last = lax.optimization_barrier((*far, *near, turned))[:2]
        crossed = [swap(v, "c") for v in last]
        pieces = own + others[:2] + up + [others[2], near[0]] + down + [others[3], near[1]]
        pieces += far + crossed

    with jax.named_scope("update"):
        send = after(send, *far, turned)
        both = (keep.astype(F32) + swap(send, "c").astype(F32)).astype(BF)
        both = after(both, *crossed)
        stacked = lax.all_to_all(both, "z", 0, 0)
        total = jnp.sum(stacked.astype(F32), axis=0)
        left, right = total[:, :256], total[:, 256:]
        same = yh == yl
        one = jnp.where(same, left, right)
        two = jnp.where(same, right, left)
        pairs = [(i, j) for i in range(2) for j in range(2)]
        one = lax.ppermute(one, ("yh", "yl"), [(i * 2 + j, j * 2 + i) for i, j in pairs])
        two = lax.ppermute(two, ("yh", "yl"), [(i * 2 + j, j * 2 + (1 - i)) for i, j in pairs])
        update = (one + two) / jnp.sqrt(jnp.float32(POP))

    with jax.named_scope("rollout"):
        done = rollout(ids, pieces, [got, turned])
    with jax.named_scope("states_back"):
        back = [done[0]] + [col_shift(done[k], dy, -dx) for k, (dy, dx) in enumerate(SHIFTS) if k > 0]
        final = join_members(ids, back)
    return final, update


def solution(mesh):
    fine = Mesh(mesh.devices.reshape(2, 8, 2, 2, 4), POP_AXES + COL_AXES)
    both = P(POP_AXES, COL_AXES)
    return jax.shard_map(
        local,
        mesh=fine,
        in_specs=(both, P(None, COL_AXES), both, both, P(POP_AXES)),
        out_specs=(both, both),
        check_vma=False,
    )
```

```python
import jax
import jax.numpy as jnp
from jax import lax
from jax.experimental import pallas as pl
from jax.experimental.pallas import tpu as pltpu
from jax.sharding import Mesh, PartitionSpec as P

STEPS = 4
SCALE = 0.02
POP = 32768
POP_AXES = ("yh", "z", "c")
COL_AXES = ("yl", "x")
SHIFTS = [(dy, dx) for dy in range(2) for dx in range(4)]
BF = jnp.bfloat16
F32 = jnp.float32


def col_shift(v, dy, dx):
    perm = []
    for yl in range(2):
        for x in range(4):
            perm.append((yl * 4 + x, (yl ^ dy) * 4 + (x + dx) % 4))
    return lax.ppermute(v, COL_AXES, perm)


def shift(v, axis, d):
    n = 8 if axis == "z" else 4
    return lax.ppermute(v, axis, [(i, (i + d) % n) for i in range(n)])


def over_x(v):
    return lax.all_to_all(v, "x", 0, 0)


def swap(v, axis):
    return lax.ppermute(v, axis, [(0, 1), (1, 0)])


def after(v, *deps):
    return lax.optimization_barrier((v,) + deps)[0]


def rows_of(block):
    return pl.ds(pl.multiple_of(block * 128, 128), 128)


def cost(us):
    return pl.CostEstimate(flops=int(us * 1.15e9), bytes_accessed=0, transcendentals=0)


def split_kernel(ids_ref, s_ref, a_ref, b_ref, o_ref, out_ref):
    yl = ids_ref[3]
    for k in range(4):
        mine, other = rows_of(yl * 4 + k), rows_of((1 - yl) * 4 + k)
        for n, (src, rows) in enumerate(
            ((s_ref, mine), (a_ref, mine), (b_ref, mine), (o_ref, mine), (s_ref, other), (a_ref, other))
        ):
            out_ref[k, n] = src[rows, :]


def split_members(ids, states, a, b, other):
    return pl.pallas_call(
        split_kernel,
        out_shape=jax.ShapeDtypeStruct((4, 6, 128, 256), BF),
        in_specs=[pl.BlockSpec(memory_space=pltpu.SMEM)] + [pl.BlockSpec(memory_space=pltpu.VMEM)] * 4,
        out_specs=pl.BlockSpec(memory_space=pltpu.VMEM),
        compiler_params=pltpu.CompilerParams(vmem_limit_bytes=60 * 2**20),
        cost_estimate=cost(0.05),
        name="split_members",
    )(ids, states, a, b, other)


def rollout_kernel(ids_ref, *refs):
    pieces, (got, turned) = refs[:16], refs[16:18]
    outs = refs[18:26]
    w, x, a, b, pre, sem = refs[26:]
    z, c, yl, xx = ids_ref[1], ids_ref[2], ids_ref[3], ids_ref[4]
    copies = []

    def copy(src, dst):
        copies.append(pltpu.make_async_copy(src, dst, sem.at[len(copies)]))

    for k in range(4):
        r = lax.rem(xx - k + 4, 4)
        copy(got.at[k, 0], x.at[:, pl.ds(pl.multiple_of(r * 256, 256), 256)])
        copy(turned.at[k, 0], x.at[:, pl.ds(pl.multiple_of(r * 256 + 1024, 256), 256)])
        copy(got.at[k, 1], a.at[r])
        copy(turned.at[k, 1], a.at[r + 4])
        copy(got.at[k, 2], b.at[r])
        copy(got.at[k, 3], b.at[r + 4])
    for part in range(2):
        for i in range(part, 16, 2):
            d, core = (0, 1, -1, 2)[i // 4], (i // 2) % 2
            zz = lax.rem(z - d + 8, 4)
            cc = c if core == 0 else 1 - c
            r = jnp.where(zz // 2 == yl, 0, 4) + lax.rem(xx - zz * 2 - cc + 8, 4)
            copy(pieces[i], w.at[slice(4 * part, 4 * part + 4), pl.ds(pl.multiple_of(r * 256, 256), 256)])
    for cp in copies:
        cp.start()

    def multiply(cur, blocks):
        for r in blocks:
            pre[:, r * 256:(r + 1) * 256] = jnp.dot(cur, w[r], preferred_element_type=F32)

    def gain_of(cur):
        dots = jnp.zeros((128, 1), F32)
        for r in range(8):
            block = cur[:, r * 256:(r + 1) * 256].astype(F32)
            dots += jnp.sum(block * a[r].astype(F32), axis=1, keepdims=True)
        return SCALE * dots

    def finish(gain):
        for r in range(8):
            cols = slice(r * 256, (r + 1) * 256)
            x[:, cols] = jnp.tanh(pre[:, cols] + gain * b[r].astype(F32)).astype(BF)

    for cp in copies[:24]:
        cp.wait()
    cur = x[...]
    gain = gain_of(cur)
    for cp in copies[24:32]:
        cp.wait()
    multiply(cur, range(4))
    for cp in copies[32:]:
        cp.wait()
    multiply(cur, range(4, 8))
    finish(gain)

    def step(_, carry):
        cur = x[...]
        gain = gain_of(cur)
        multiply(cur, range(8))
        finish(gain)
        return carry

    lax.fori_loop(1, STEPS, step, 0)
    for k in range(8):
        outs[k][...] = x[:, k * 256:(k + 1) * 256]


def rollout(ids, pieces, members):
    return pl.pallas_call(
        rollout_kernel,
        out_shape=[jax.ShapeDtypeStruct((128, 256), BF)] * 8,
        in_specs=[pl.BlockSpec(memory_space=pltpu.SMEM)] + [pl.BlockSpec(memory_space=pl.ANY)] * 18,
        out_specs=[pl.BlockSpec(memory_space=pltpu.VMEM)] * 8,
        scratch_shapes=[
            pltpu.VMEM((8, 2048, 256), BF),
            pltpu.VMEM((128, 2048), BF),
            pltpu.VMEM((8, 128, 256), BF),
            pltpu.VMEM((8, 128, 256), BF),
            pltpu.VMEM((128, 2048), F32),
            pltpu.SemaphoreType.DMA((40,)),
        ],
        compiler_params=pltpu.CompilerParams(vmem_limit_bytes=60 * 2**20),
        cost_estimate=cost(0.05),
        name="rollout",
    )(ids, *pieces, *members)


def update_kernel(ids_ref, all_ref, fit_ref, a0, a1, a2, lo, hi, b0, b1, keep_ref, send_ref):
    first = ids_ref[2] == 0
    x = ids_ref[4]
    where = [lax.rem(x + d, 4) for d in (0, 3, 1, 2)]
    mean = jnp.sum(all_ref[...], keepdims=True).reshape(1, 1) / POP
    var = jnp.sum((all_ref[...] - mean) ** 2, keepdims=True).reshape(1, 1) / POP
    norm = (fit_ref[...] - mean) / jnp.sqrt(var + 1e-05)
    for k, a in enumerate((a0, a1, a2, lo, hi)):
        scaled = (norm * a[...].astype(F32)).astype(BF)
        n = scaled.shape[1] // 128
        row = 2 * where[min(k, 3)] + (1 if k == 4 else 0)
        for h, b in enumerate((b0, b1)):
            d = lax.dot_general(scaled, b[...], (((0,), (0,)), ((), ())), preferred_element_type=F32)
            d = d.reshape(n, 2, 64, 256).astype(BF)
            cols = slice(h * 256, (h + 1) * 256)
            keep_ref[pl.ds(row, n), :, cols] = jnp.where(first, d[:, 0], d[:, 1])
            send_ref[pl.ds(row, n), :, cols] = jnp.where(first, d[:, 1], d[:, 0])


def partial_update(ids, everyone, fitness, a, b):
    shape = jax.ShapeDtypeStruct((8, 64, 512), BF)
    return pl.pallas_call(
        update_kernel,
        out_shape=[shape, shape],
        in_specs=[pl.BlockSpec(memory_space=pltpu.SMEM)] + [pl.BlockSpec(memory_space=pltpu.VMEM)] * 9,
        out_specs=[pl.BlockSpec(memory_space=pltpu.VMEM)] * 2,
        compiler_params=pltpu.CompilerParams(vmem_limit_bytes=60 * 2**20),
        cost_estimate=cost(0.05),
        name="partial_update",
    )(ids, everyone, fitness, *a, *b)


def join_kernel(ids_ref, *refs):
    pieces, out_ref = refs[:8], refs[8]
    yl, x = ids_ref[3], ids_ref[4]
    for k, (dy, dx) in enumerate(SHIFTS):
        block = (yl if dy == 0 else 1 - yl) * 4 + lax.rem(x + dx, 4)
        out_ref[rows_of(block), :] = pieces[k][...]


def join_members(ids, pieces):
    return pl.pallas_call(
        join_kernel,
        out_shape=jax.ShapeDtypeStruct((1024, 256), BF),
        in_specs=[pl.BlockSpec(memory_space=pltpu.SMEM)] + [pl.BlockSpec(memory_space=pltpu.VMEM)] * 8,
        out_specs=pl.BlockSpec(memory_space=pltpu.VMEM),
        compiler_params=pltpu.CompilerParams(vmem_limit_bytes=60 * 2**20),
        name="join_members",
    )(ids, *pieces)


def local(states, weight, noise_in, noise_out, fitness):
    yh, z, c = (lax.axis_index(n) for n in POP_AXES)
    yl, x = (lax.axis_index(n) for n in COL_AXES)
    ids = jnp.stack([yh, z, c, yl, x]).astype(jnp.int32)

    with jax.named_scope("weight_rows"):
        share = lax.dynamic_slice_in_dim(weight, (z % 4) * 512 + c * 256, 256, 0)
        own = [jnp.stack([share] + [shift(share, "x", dx) for dx in (1, 2, 3)])]
        b = [noise_out, swap(noise_out, "yl")]
        two = jnp.stack([fitness, swap(after(fitness, share), "c")])

    with jax.named_scope("round_1"):
        first, a_in, two = lax.optimization_barrier((own[0], noise_in, two))
        own.append(swap(first, "yl"))
        up, down = [shift(first, "z", 1)], [shift(first, "z", -1)]
        left, right = shift(a_in, "x", 1), shift(a_in, "x", -1)
        parts = split_members(ids, states, noise_in, *b)

    with jax.named_scope("round_2"):
        others = [swap(v, "c") for v in (*own, up[0], down[0])]
        second, left, right, two = lax.optimization_barrier((own[1], left, right, two, *others))[:4]
        four = jnp.stack([two, swap(two, "yh")])
        up.append(shift(second, "z", 1))
        down.append(shift(second, "z", -1))
        got = over_x(after(parts, first))

    with jax.named_scope("round_3"):
        a = [noise_in, left, right, shift(left[:, :128], "x", 1), shift(right[:, 128:], "x", -1)]
        fore, back, turn, four = lax.optimization_barrier(
            (up[0], down[1], got[:, 4:], four, up[1], a[3], a[4])
        )[:4]
        far = [shift(fore, "z", 1), shift(back, "z", -1)]
        turned = swap(turn, "yl")
        everyone = lax.all_to_all(jnp.broadcast_to(four.reshape(1, 32, 128), (8, 32, 128)), "z", 0, 0)
        near = [swap(v, "c") for v in (up[1], down[1])]
        keep, send = partial_update(ids, everyone, fitness.reshape(1024, 1), a, b)

    with jax.named_scope("weight"):
        last = lax.optimization_barrier((*far, *near, turned))[:2]
        crossed = [swap(v, "c") for v in last]
        pieces = own + others[:2] + up + [others[2], near[0]] + down + [others[3], near[1]]
        pieces += far + crossed

    with jax.named_scope("update"):
        send = after(send, *far, turned)
        both = (keep.astype(F32) + swap(send, "c").astype(F32)).astype(BF)
        both = after(both, *crossed)
        stacked = lax.all_to_all(both, "z", 0, 0)
        total = jnp.sum(stacked.astype(F32), axis=0)
        left, right = total[:, :256], total[:, 256:]
        same = yh == yl
        one = jnp.where(same, left, right)
        two = jnp.where(same, right, left)
        pairs = [(i, j) for i in range(2) for j in range(2)]
        one = lax.ppermute(one, ("yh", "yl"), [(i * 2 + j, j * 2 + i) for i, j in pairs])
        two = lax.ppermute(two, ("yh", "yl"), [(i * 2 + j, j * 2 + (1 - i)) for i, j in pairs])
        update = (one + two) / jnp.sqrt(jnp.float32(POP))

    with jax.named_scope("rollout"):
        done = rollout(ids, pieces, [got, turned])
    with jax.named_scope("states_back"):
        back = [done[0]] + [col_shift(done[k], dy, -dx) for k, (dy, dx) in enumerate(SHIFTS) if k > 0]
        final = join_members(ids, back)
    return final, update


def solution(mesh):
    fine = Mesh(mesh.devices.reshape(2, 8, 2, 2, 4), POP_AXES + COL_AXES)
    both = P(POP_AXES, COL_AXES)
    return jax.shard_map(
        local,
        mesh=fine,
        in_specs=(both, P(None, COL_AXES), both, both, P(POP_AXES)),
        out_specs=(both, both),
        check_vma=False,
    )
```

```python
import jax
import jax.numpy as jnp
from jax import lax
from jax.experimental import pallas as pl
from jax.experimental.pallas import tpu as pltpu
from jax.sharding import Mesh, PartitionSpec as P

STEPS = 4
SCALE = 0.02
POP = 32768
POP_AXES = ("yh", "z", "c")
COL_AXES = ("yl", "x")
SHIFTS = [(dy, dx) for dy in range(2) for dx in range(4)]
BF = jnp.bfloat16
F32 = jnp.float32


def col_shift(v, dy, dx):
    perm = []
    for yl in range(2):
        for x in range(4):
            perm.append((yl * 4 + x, (yl ^ dy) * 4 + (x + dx) % 4))
    return lax.ppermute(v, COL_AXES, perm)


def shift(v, axis, d):
    n = 8 if axis == "z" else 4
    return lax.ppermute(v, axis, [(i, (i + d) % n) for i in range(n)])


def over_x(v):
    return lax.all_to_all(v, "x", 0, 0)


def swap(v, axis):
    return lax.ppermute(v, axis, [(0, 1), (1, 0)])


def after(v, *deps):
    return lax.optimization_barrier((v,) + deps)[0]


def rows_of(block):
    return pl.ds(pl.multiple_of(block * 128, 128), 128)


def cost(us):
    return pl.CostEstimate(flops=int(us * 1.15e9), bytes_accessed=0, transcendentals=0)


def split_kernel(ids_ref, s_ref, a_ref, b_ref, o_ref, out_ref):
    yl = ids_ref[3]
    for k in range(4):
        mine, other = rows_of(yl * 4 + k), rows_of((1 - yl) * 4 + k)
        for n, (src, rows) in enumerate(
            ((s_ref, mine), (a_ref, mine), (b_ref, mine), (o_ref, mine), (s_ref, other), (a_ref, other))
        ):
            out_ref[k, n] = src[rows, :]


def split_members(ids, states, a, b, other):
    return pl.pallas_call(
        split_kernel,
        out_shape=jax.ShapeDtypeStruct((4, 6, 128, 256), BF),
        in_specs=[pl.BlockSpec(memory_space=pltpu.SMEM)] + [pl.BlockSpec(memory_space=pltpu.VMEM)] * 4,
        out_specs=pl.BlockSpec(memory_space=pltpu.VMEM),
        compiler_params=pltpu.CompilerParams(vmem_limit_bytes=60 * 2**20),
        cost_estimate=cost(0.05),
        name="split_members",
    )(ids, states, a, b, other)


def rollout_kernel(ids_ref, *refs):
    pieces, (got, turned) = refs[:16], refs[16:18]
    outs = refs[18:26]
    w, x, a, b, pre, sem = refs[26:]
    z, c, yl, xx = ids_ref[1], ids_ref[2], ids_ref[3], ids_ref[4]
    copies = []

    def copy(src, dst):
        copies.append(pltpu.make_async_copy(src, dst, sem.at[len(copies)]))

    for k in range(4):
        r = lax.rem(xx - k + 4, 4)
        copy(got.at[k, 0], x.at[:, pl.ds(pl.multiple_of(r * 256, 256), 256)])
        copy(turned.at[k, 0], x.at[:, pl.ds(pl.multiple_of(r * 256 + 1024, 256), 256)])
        copy(got.at[k, 1], a.at[r])
        copy(turned.at[k, 1], a.at[r + 4])
        copy(got.at[k, 2], b.at[r])
        copy(got.at[k, 3], b.at[r + 4])
    for part in range(2):
        for i in range(part, 16, 2):
            d, core = (0, 1, -1, 2)[i // 4], (i // 2) % 2
            zz = lax.rem(z - d + 8, 4)
            cc = c if core == 0 else 1 - c
            r = jnp.where(zz // 2 == yl, 0, 4) + lax.rem(xx - zz * 2 - cc + 8, 4)
            copy(pieces[i], w.at[slice(4 * part, 4 * part + 4), pl.ds(pl.multiple_of(r * 256, 256), 256)])
    for cp in copies:
        cp.start()

    def multiply(cur, blocks):
        for r in blocks:
            pre[:, r * 256:(r + 1) * 256] = jnp.dot(cur, w[r], preferred_element_type=F32)

    def gain_of(cur):
        dots = jnp.zeros((128, 1), F32)
        for r in range(8):
            block = cur[:, r * 256:(r + 1) * 256].astype(F32)
            dots += jnp.sum(block * a[r].astype(F32), axis=1, keepdims=True)
        return SCALE * dots

    def finish(gain):
        for r in range(8):
            cols = slice(r * 256, (r + 1) * 256)
            x[:, cols] = jnp.tanh(pre[:, cols] + gain * b[r].astype(F32)).astype(BF)

    for cp in copies[:24]:
        cp.wait()
    cur = x[...]
    gain = gain_of(cur)
    for cp in copies[24:32]:
        cp.wait()
    multiply(cur, range(4))
    for cp in copies[32:]:
        cp.wait()
    multiply(cur, range(4, 8))
    finish(gain)

    def step(_, carry):
        cur = x[...]
        gain = gain_of(cur)
        multiply(cur, range(8))
        finish(gain)
        return carry

    lax.fori_loop(1, STEPS, step, 0)
    for k in range(8):
        outs[k][...] = x[:, k * 256:(k + 1) * 256]


def rollout(ids, pieces, members):
    return pl.pallas_call(
        rollout_kernel,
        out_shape=[jax.ShapeDtypeStruct((128, 256), BF)] * 8,
        in_specs=[pl.BlockSpec(memory_space=pltpu.SMEM)] + [pl.BlockSpec(memory_space=pl.ANY)] * 18,
        out_specs=[pl.BlockSpec(memory_space=pltpu.VMEM)] * 8,
        scratch_shapes=[
            pltpu.VMEM((8, 2048, 256), BF),
            pltpu.VMEM((128, 2048), BF),
            pltpu.VMEM((8, 128, 256), BF),
            pltpu.VMEM((8, 128, 256), BF),
            pltpu.VMEM((128, 2048), F32),
            pltpu.SemaphoreType.DMA((40,)),
        ],
        compiler_params=pltpu.CompilerParams(vmem_limit_bytes=60 * 2**20),
        cost_estimate=cost(0.05),
        name="rollout",
    )(ids, *pieces, *members)


def update_kernel(ids_ref, all_ref, fit_ref, a0, a1, a2, lo, hi, b0, b1, keep_ref, send_ref):
    first = ids_ref[2] == 0
    x = ids_ref[4]
    where = [lax.rem(x + d, 4) for d in (0, 3, 1, 2)]
    mean = jnp.sum(all_ref[...], keepdims=True).reshape(1, 1) / POP
    var = jnp.sum((all_ref[...] - mean) ** 2, keepdims=True).reshape(1, 1) / POP
    norm = (fit_ref[...] - mean) / jnp.sqrt(var + 1e-05)
    for k, a in enumerate((a0, a1, a2, lo, hi)):
        scaled = (norm * a[...].astype(F32)).astype(BF)
        n = scaled.shape[1] // 128
        row = 2 * where[min(k, 3)] + (1 if k == 4 else 0)
        for h, b in enumerate((b0, b1)):
            d = lax.dot_general(scaled, b[...], (((0,), (0,)), ((), ())), preferred_element_type=F32)
            d = d.reshape(n, 2, 64, 256).astype(BF)
            cols = slice(h * 256, (h + 1) * 256)
            keep_ref[pl.ds(row, n), :, cols] = jnp.where(first, d[:, 0], d[:, 1])
            send_ref[pl.ds(row, n), :, cols] = jnp.where(first, d[:, 1], d[:, 0])


def partial_update(ids, everyone, fitness, a, b):
    shape = jax.ShapeDtypeStruct((8, 64, 512), BF)
    return pl.pallas_call(
        update_kernel,
        out_shape=[shape, shape],
        in_specs=[pl.BlockSpec(memory_space=pltpu.SMEM)] + [pl.BlockSpec(memory_space=pltpu.VMEM)] * 9,
        out_specs=[pl.BlockSpec(memory_space=pltpu.VMEM)] * 2,
        compiler_params=pltpu.CompilerParams(vmem_limit_bytes=60 * 2**20),
        cost_estimate=cost(0.05),
        name="partial_update",
    )(ids, everyone, fitness, *a, *b)


def join_kernel(ids_ref, *refs):
    pieces, out_ref = refs[:8], refs[8]
    yl, x = ids_ref[3], ids_ref[4]
    for k, (dy, dx) in enumerate(SHIFTS):
        block = (yl if dy == 0 else 1 - yl) * 4 + lax.rem(x + dx, 4)
        out_ref[rows_of(block), :] = pieces[k][...]


def join_members(ids, pieces):
    return pl.pallas_call(
        join_kernel,
        out_shape=jax.ShapeDtypeStruct((1024, 256), BF),
        in_specs=[pl.BlockSpec(memory_space=pltpu.SMEM)] + [pl.BlockSpec(memory_space=pltpu.VMEM)] * 8,
        out_specs=pl.BlockSpec(memory_space=pltpu.VMEM),
        compiler_params=pltpu.CompilerParams(vmem_limit_bytes=60 * 2**20),
        name="join_members",
    )(ids, *pieces)


def local(states, weight, noise_in, noise_out, fitness):
    yh, z, c = (lax.axis_index(n) for n in POP_AXES)
    yl, x = (lax.axis_index(n) for n in COL_AXES)
    ids = jnp.stack([yh, z, c, yl, x]).astype(jnp.int32)

    with jax.named_scope("fitness"):
        along_z = lax.all_to_all(jnp.broadcast_to(fitness.reshape(1, 8, 128), (8, 8, 128)), "z", 0, 0)

    with jax.named_scope("weight_rows"):
        share = lax.dynamic_slice_in_dim(weight, (z % 4) * 512 + c * 256, 256, 0)
        own = [jnp.stack([share] + [shift(share, "x", dx) for dx in (1, 2, 3)])]
        b = [noise_out, swap(noise_out, "yl")]

    with jax.named_scope("round_1"):
        first, a_in = lax.optimization_barrier((own[0], noise_in, along_z))[:2]
        own.append(swap(after(first, b[1]), "yl"))
        up, down = [shift(first, "z", 1)], [shift(first, "z", -1)]
        left, right = shift(a_in, "x", 1), shift(a_in, "x", -1)
        parts = split_members(ids, states, noise_in, *b)

    with jax.named_scope("round_2"):
        others = [swap(v, "c") for v in (*own, up[0], down[0])]
        second, along_z = lax.optimization_barrier((own[1], along_z, *others))[:2]
        up.append(shift(second, "z", 1))
        down.append(shift(second, "z", -1))
        got = over_x(after(parts, first))
        pair = jnp.stack([along_z, swap(along_z, "c")])
        everyone = jnp.stack([pair, swap(pair, "yh")]).reshape(32, 8, 128)

    with jax.named_scope("round_3"):
        fore, back, turn = lax.optimization_barrier((up[0], down[1], got[:, 4:], up[1], everyone))[:3]
        left, right = lax.optimization_barrier((left, right, up[1], down[1]))[:2]
        far = [shift(fore, "z", 1), shift(back, "z", -1)]
        turned = swap(turn, "yl")
        a = [noise_in, left, right, shift(left[:, :128], "x", 1), shift(right[:, 128:], "x", -1)]
        near = [swap(v, "c") for v in (up[1], down[1])]
        keep, send = partial_update(ids, everyone, fitness.reshape(1024, 1), a, b)

    with jax.named_scope("weight"):
        last = lax.optimization_barrier((*far, *near, turned))[:2]
        crossed = [swap(v, "c") for v in last]
        pieces = own + others[:2] + up + [others[2], near[0]] + down + [others[3], near[1]]
        pieces += far + crossed

    with jax.named_scope("update"):
        send = after(send, *far, turned)
        both = (keep.astype(F32) + swap(send, "c").astype(F32)).astype(BF)
        both = after(both, *crossed)
        stacked = lax.all_to_all(both, "z", 0, 0)
        total = jnp.sum(stacked.astype(F32), axis=0)
        left, right = total[:, :256], total[:, 256:]
        same = yh == yl
        one = jnp.where(same, left, right)
        two = jnp.where(same, right, left)
        pairs = [(i, j) for i in range(2) for j in range(2)]
        one = lax.ppermute(one, ("yh", "yl"), [(i * 2 + j, j * 2 + i) for i, j in pairs])
        two = lax.ppermute(two, ("yh", "yl"), [(i * 2 + j, j * 2 + (1 - i)) for i, j in pairs])
        update = (one + two) / jnp.sqrt(jnp.float32(POP))

    with jax.named_scope("rollout"):
        done = rollout(ids, pieces, [got, turned])
    with jax.named_scope("states_back"):
        back = [done[0]] + [col_shift(done[k], dy, -dx) for k, (dy, dx) in enumerate(SHIFTS) if k > 0]
        final = join_members(ids, back)
    return final, update


def solution(mesh):
    fine = Mesh(mesh.devices.reshape(2, 8, 2, 2, 4), POP_AXES + COL_AXES)
    both = P(POP_AXES, COL_AXES)
    return jax.shard_map(
        local,
        mesh=fine,
        in_specs=(both, P(None, COL_AXES), both, both, P(POP_AXES)),
        out_specs=(both, both),
        check_vma=False,
    )
```

```python
import jax
import jax.numpy as jnp
from jax import lax
from jax.experimental import pallas as pl
from jax.experimental.pallas import tpu as pltpu
from jax.sharding import Mesh, PartitionSpec as P

STEPS = 4
SCALE = 0.02
POP = 32768
POP_AXES = ("yh", "z", "c")
COL_AXES = ("yl", "x")
SHIFTS = [(dy, dx) for dy in range(2) for dx in range(4)]
BF = jnp.bfloat16
F32 = jnp.float32


def col_shift(v, dy, dx):
    perm = []
    for yl in range(2):
        for x in range(4):
            perm.append((yl * 4 + x, (yl ^ dy) * 4 + (x + dx) % 4))
    return lax.ppermute(v, COL_AXES, perm)


def shift(v, axis, d):
    n = 8 if axis == "z" else 4
    return lax.ppermute(v, axis, [(i, (i + d) % n) for i in range(n)])


def over_x(v):
    return lax.all_to_all(v, "x", 0, 0)


def swap(v, axis):
    return lax.ppermute(v, axis, [(0, 1), (1, 0)])


def after(v, *deps):
    return lax.optimization_barrier((v,) + deps)[0]


def rows_of(block):
    return pl.ds(pl.multiple_of(block * 128, 128), 128)


def cost(us):
    return pl.CostEstimate(flops=int(us * 1.15e9), bytes_accessed=0, transcendentals=0)


def split_kernel(ids_ref, s_ref, a_ref, b_ref, o_ref, out_ref):
    yl = ids_ref[3]
    for k in range(4):
        mine, other = rows_of(yl * 4 + k), rows_of((1 - yl) * 4 + k)
        for n, (src, rows) in enumerate(
            ((s_ref, mine), (a_ref, mine), (b_ref, mine), (o_ref, mine), (s_ref, other), (a_ref, other))
        ):
            out_ref[k, n] = src[rows, :]


def split_members(ids, states, a, b, other):
    return pl.pallas_call(
        split_kernel,
        out_shape=jax.ShapeDtypeStruct((4, 6, 128, 256), BF),
        in_specs=[pl.BlockSpec(memory_space=pltpu.SMEM)] + [pl.BlockSpec(memory_space=pltpu.VMEM)] * 4,
        out_specs=pl.BlockSpec(memory_space=pltpu.VMEM),
        compiler_params=pltpu.CompilerParams(vmem_limit_bytes=60 * 2**20),
        cost_estimate=cost(0.05),
        name="split_members",
    )(ids, states, a, b, other)


def rollout_kernel(ids_ref, *refs):
    pieces, (got, turned) = refs[:16], refs[16:18]
    outs = refs[18:26]
    w, x, a, b, pre, sem = refs[26:]
    z, c, yl, xx = ids_ref[1], ids_ref[2], ids_ref[3], ids_ref[4]
    copies = []

    def copy(src, dst):
        copies.append(pltpu.make_async_copy(src, dst, sem.at[len(copies)]))

    for k in range(4):
        r = lax.rem(xx - k + 4, 4)
        copy(got.at[k, 0], x.at[:, pl.ds(pl.multiple_of(r * 256, 256), 256)])
        copy(turned.at[k, 0], x.at[:, pl.ds(pl.multiple_of(r * 256 + 1024, 256), 256)])
        copy(got.at[k, 1], a.at[r])
        copy(turned.at[k, 1], a.at[r + 4])
        copy(got.at[k, 2], b.at[r])
        copy(got.at[k, 3], b.at[r + 4])
    for part in range(2):
        for i in range(part, 16, 2):
            d, core = (0, 1, -1, 2)[i // 4], (i // 2) % 2
            zz = lax.rem(z - d + 8, 4)
            cc = c if core == 0 else 1 - c
            r = jnp.where(zz // 2 == yl, 0, 4) + lax.rem(xx - zz * 2 - cc + 8, 4)
            copy(pieces[i], w.at[slice(4 * part, 4 * part + 4), pl.ds(pl.multiple_of(r * 256, 256), 256)])
    for cp in copies:
        cp.start()

    def multiply(cur, blocks):
        for r in blocks:
            pre[:, r * 256:(r + 1) * 256] = jnp.dot(cur, w[r], preferred_element_type=F32)

    def gain_of(cur):
        dots = jnp.zeros((128, 1), F32)
        for r in range(8):
            block = cur[:, r * 256:(r + 1) * 256].astype(F32)
            dots += jnp.sum(block * a[r].astype(F32), axis=1, keepdims=True)
        return SCALE * dots

    def finish(gain):
        for r in range(8):
            cols = slice(r * 256, (r + 1) * 256)
            x[:, cols] = jnp.tanh(pre[:, cols] + gain * b[r].astype(F32)).astype(BF)

    for cp in copies[:24]:
        cp.wait()
    cur = x[...]
    gain = gain_of(cur)
    for cp in copies[24:32]:
        cp.wait()
    multiply(cur, range(4))
    for cp in copies[32:]:
        cp.wait()
    multiply(cur, range(4, 8))
    finish(gain)

    def step(_, carry):
        cur = x[...]
        gain = gain_of(cur)
        multiply(cur, range(8))
        finish(gain)
        return carry

    lax.fori_loop(1, STEPS, step, 0)
    for k in range(8):
        outs[k][...] = x[:, k * 256:(k + 1) * 256]


def rollout(ids, pieces, members):
    return pl.pallas_call(
        rollout_kernel,
        out_shape=[jax.ShapeDtypeStruct((128, 256), BF)] * 8,
        in_specs=[pl.BlockSpec(memory_space=pltpu.SMEM)] + [pl.BlockSpec(memory_space=pl.ANY)] * 18,
        out_specs=[pl.BlockSpec(memory_space=pltpu.VMEM)] * 8,
        scratch_shapes=[
            pltpu.VMEM((8, 2048, 256), BF),
            pltpu.VMEM((128, 2048), BF),
            pltpu.VMEM((8, 128, 256), BF),
            pltpu.VMEM((8, 128, 256), BF),
            pltpu.VMEM((128, 2048), F32),
            pltpu.SemaphoreType.DMA((40,)),
        ],
        compiler_params=pltpu.CompilerParams(vmem_limit_bytes=60 * 2**20),
        cost_estimate=cost(0.05),
        name="rollout",
    )(ids, *pieces, *members)


def update_kernel(ids_ref, all_ref, fit_ref, a0, a1, a2, lo, hi, b0, b1, keep_ref, send_ref):
    first = ids_ref[2] == 0
    x = ids_ref[4]
    where = [lax.rem(x + d, 4) for d in (0, 3, 1, 2)]
    mean = jnp.sum(all_ref[...], keepdims=True).reshape(1, 1) / POP
    var = jnp.sum((all_ref[...] - mean) ** 2, keepdims=True).reshape(1, 1) / POP
    norm = (fit_ref[...] - mean) / jnp.sqrt(var + 1e-05)
    for k, a in enumerate((a0, a1, a2, lo, hi)):
        scaled = (norm * a[...].astype(F32)).astype(BF)
        n = scaled.shape[1] // 128
        row = 2 * where[min(k, 3)] + (1 if k == 4 else 0)
        for h, b in enumerate((b0, b1)):
            d = lax.dot_general(scaled, b[...], (((0,), (0,)), ((), ())), preferred_element_type=F32)
            d = d.reshape(n, 2, 64, 256).astype(BF)
            cols = slice(h * 256, (h + 1) * 256)
            keep_ref[pl.ds(row, n), :, cols] = jnp.where(first, d[:, 0], d[:, 1])
            send_ref[pl.ds(row, n), :, cols] = jnp.where(first, d[:, 1], d[:, 0])


def partial_update(ids, everyone, fitness, a, b):
    shape = jax.ShapeDtypeStruct((8, 64, 512), BF)
    return pl.pallas_call(
        update_kernel,
        out_shape=[shape, shape],
        in_specs=[pl.BlockSpec(memory_space=pltpu.SMEM)] + [pl.BlockSpec(memory_space=pltpu.VMEM)] * 9,
        out_specs=[pl.BlockSpec(memory_space=pltpu.VMEM)] * 2,
        compiler_params=pltpu.CompilerParams(vmem_limit_bytes=60 * 2**20),
        cost_estimate=cost(0.05),
        name="partial_update",
    )(ids, everyone, fitness, *a, *b)


def join_kernel(ids_ref, *refs):
    pieces, out_ref = refs[:8], refs[8]
    yl, x = ids_ref[3], ids_ref[4]
    for k, (dy, dx) in enumerate(SHIFTS):
        block = (yl if dy == 0 else 1 - yl) * 4 + lax.rem(x + dx, 4)
        out_ref[rows_of(block), :] = pieces[k][...]


def join_members(ids, pieces):
    return pl.pallas_call(
        join_kernel,
        out_shape=jax.ShapeDtypeStruct((1024, 256), BF),
        in_specs=[pl.BlockSpec(memory_space=pltpu.SMEM)] + [pl.BlockSpec(memory_space=pltpu.VMEM)] * 8,
        out_specs=pl.BlockSpec(memory_space=pltpu.VMEM),
        compiler_params=pltpu.CompilerParams(vmem_limit_bytes=60 * 2**20),
        name="join_members",
    )(ids, *pieces)


def local(states, weight, noise_in, noise_out, fitness):
    yh, z, c = (lax.axis_index(n) for n in POP_AXES)
    yl, x = (lax.axis_index(n) for n in COL_AXES)
    ids = jnp.stack([yh, z, c, yl, x]).astype(jnp.int32)

    with jax.named_scope("fitness"):
        along_z = lax.all_to_all(jnp.broadcast_to(fitness.reshape(1, 8, 128), (8, 8, 128)), "z", 0, 0)

    with jax.named_scope("weight_rows"):
        share = lax.dynamic_slice_in_dim(weight, (z % 4) * 512 + c * 256, 256, 0)
        own = [jnp.stack([share] + [shift(share, "x", dx) for dx in (1, 2, 3)])]
        b = [noise_out, swap(noise_out, "yl")]

    with jax.named_scope("round_1"):
        first = own[0]
        own.append(swap(after(first, b[1]), "yl"))
        up, down = [shift(first, "z", 1)], [shift(first, "z", -1)]
        left, right = shift(noise_in, "x", 1), shift(noise_in, "x", -1)
        parts = split_members(ids, states, noise_in, *b)

    with jax.named_scope("round_2"):
        others = [swap(v, "c") for v in (own[0], after(own[1], left, right, along_z), up[0], down[0])]
        second, along_z = lax.optimization_barrier((own[1], along_z, *others))[:2]
        up.append(shift(second, "z", 1))
        down.append(shift(second, "z", -1))
        got = over_x(after(parts, first))
        pair = jnp.stack([along_z, swap(along_z, "c")])
        everyone = jnp.stack([pair, swap(pair, "yh")]).reshape(32, 8, 128)

    with jax.named_scope("round_3"):
        fore, back = lax.optimization_barrier((up[0], down[1], up[1], everyone))[:2]
        turn = lax.optimization_barrier((got[:, 4:], up[1], down[1]))[0]
        far = [shift(fore, "z", 1), shift(back, "z", -1)]
        turned = swap(turn, "yl")
        a = [noise_in, left, right, shift(left[:, :128], "x", 1), shift(right[:, 128:], "x", -1)]
        near = [swap(v, "c") for v in (up[1], down[1])]
        keep, send = partial_update(ids, everyone, fitness.reshape(1024, 1), a, b)

    with jax.named_scope("weight"):
        last = lax.optimization_barrier((*far, *near, turned))[:2]
        crossed = [swap(v, "c") for v in last]
        pieces = own + others[:2] + up + [others[2], near[0]] + down + [others[3], near[1]]
        pieces += far + crossed

    with jax.named_scope("update"):
        both = (keep.astype(F32) + swap(send, "c").astype(F32)).astype(BF)
        both = after(both, *crossed)
        stacked = lax.all_to_all(both, "z", 0, 0)
        total = jnp.sum(stacked.astype(F32), axis=0)
        left, right = total[:, :256], total[:, 256:]
        same = yh == yl
        one = jnp.where(same, left, right)
        two = jnp.where(same, right, left)
        pairs = [(i, j) for i in range(2) for j in range(2)]
        one = lax.ppermute(one, ("yh", "yl"), [(i * 2 + j, j * 2 + i) for i, j in pairs])
        two = lax.ppermute(two, ("yh", "yl"), [(i * 2 + j, j * 2 + (1 - i)) for i, j in pairs])
        update = (one + two) / jnp.sqrt(jnp.float32(POP))

    with jax.named_scope("rollout"):
        done = rollout(ids, pieces, [got, turned])
    with jax.named_scope("states_back"):
        back = [done[0]] + [col_shift(done[k], dy, -dx) for k, (dy, dx) in enumerate(SHIFTS) if k > 0]
        final = join_members(ids, back)
    return final, update


def solution(mesh):
    fine = Mesh(mesh.devices.reshape(2, 8, 2, 2, 4), POP_AXES + COL_AXES)
    both = P(POP_AXES, COL_AXES)
    return jax.shard_map(
        local,
        mesh=fine,
        in_specs=(both, P(None, COL_AXES), both, both, P(POP_AXES)),
        out_specs=(both, both),
        check_vma=False,
    )
```

```python
import jax
import jax.numpy as jnp
from jax import lax
from jax.experimental import pallas as pl
from jax.experimental.pallas import tpu as pltpu
from jax.sharding import Mesh, PartitionSpec as P

STEPS = 4
SCALE = 0.02
POP = 32768
POP_AXES = ("yh", "z", "c")
COL_AXES = ("yl", "x")
SHIFTS = [(dy, dx) for dy in range(2) for dx in range(4)]
BF = jnp.bfloat16
F32 = jnp.float32


def col_shift(v, dy, dx):
    perm = []
    for yl in range(2):
        for x in range(4):
            perm.append((yl * 4 + x, (yl ^ dy) * 4 + (x + dx) % 4))
    return lax.ppermute(v, COL_AXES, perm)


def shift(v, axis, d):
    n = 8 if axis == "z" else 4
    return lax.ppermute(v, axis, [(i, (i + d) % n) for i in range(n)])


def over_x(v):
    return lax.all_to_all(v, "x", 0, 0)


def swap(v, axis):
    return lax.ppermute(v, axis, [(0, 1), (1, 0)])


def after(v, *deps):
    return lax.optimization_barrier((v,) + deps)[0]


def rows_of(block):
    return pl.ds(pl.multiple_of(block * 128, 128), 128)


def cost(us):
    return pl.CostEstimate(flops=int(us * 1.15e9), bytes_accessed=0, transcendentals=0)


def split_kernel(ids_ref, s_ref, a_ref, b_ref, o_ref, out_ref):
    yl = ids_ref[3]
    for k in range(4):
        mine, other = rows_of(yl * 4 + k), rows_of((1 - yl) * 4 + k)
        for n, (src, rows) in enumerate(
            ((s_ref, mine), (a_ref, mine), (b_ref, mine), (o_ref, mine), (s_ref, other), (a_ref, other))
        ):
            out_ref[k, n] = src[rows, :]


def split_members(ids, states, a, b, other):
    return pl.pallas_call(
        split_kernel,
        out_shape=jax.ShapeDtypeStruct((4, 6, 128, 256), BF),
        in_specs=[pl.BlockSpec(memory_space=pltpu.SMEM)] + [pl.BlockSpec(memory_space=pltpu.VMEM)] * 4,
        out_specs=pl.BlockSpec(memory_space=pltpu.VMEM),
        compiler_params=pltpu.CompilerParams(vmem_limit_bytes=60 * 2**20),
        cost_estimate=cost(0.05),
        name="split_members",
    )(ids, states, a, b, other)


def rollout_kernel(ids_ref, *refs):
    pieces, (got, turned) = refs[:16], refs[16:18]
    outs = refs[18:26]
    w, x, a, b, pre, sem = refs[26:]
    z, c, yl, xx = ids_ref[1], ids_ref[2], ids_ref[3], ids_ref[4]
    copies = []

    def copy(src, dst):
        copies.append(pltpu.make_async_copy(src, dst, sem.at[len(copies)]))

    for k in range(4):
        r = lax.rem(xx - k + 4, 4)
        copy(got.at[k, 0], x.at[:, pl.ds(pl.multiple_of(r * 256, 256), 256)])
        copy(turned.at[k, 0], x.at[:, pl.ds(pl.multiple_of(r * 256 + 1024, 256), 256)])
        copy(got.at[k, 1], a.at[r])
        copy(turned.at[k, 1], a.at[r + 4])
        copy(got.at[k, 2], b.at[r])
        copy(got.at[k, 3], b.at[r + 4])
    for part in range(2):
        for i in range(part, 16, 2):
            d, core = (0, 1, -1, 2)[i // 4], (i // 2) % 2
            zz = lax.rem(z - d + 8, 4)
            cc = c if core == 0 else 1 - c
            r = jnp.where(zz // 2 == yl, 0, 4) + lax.rem(xx - zz * 2 - cc + 8, 4)
            copy(pieces[i], w.at[slice(4 * part, 4 * part + 4), pl.ds(pl.multiple_of(r * 256, 256), 256)])
    for cp in copies:
        cp.start()

    def multiply(cur, blocks):
        for r in blocks:
            pre[:, r * 256:(r + 1) * 256] = jnp.dot(cur, w[r], preferred_element_type=F32)

    def gain_of(cur):
        dots = jnp.zeros((128, 1), F32)
        for r in range(8):
            block = cur[:, r * 256:(r + 1) * 256].astype(F32)
            dots += jnp.sum(block * a[r].astype(F32), axis=1, keepdims=True)
        return SCALE * dots

    def finish(gain):
        for r in range(8):
            cols = slice(r * 256, (r + 1) * 256)
            x[:, cols] = jnp.tanh(pre[:, cols] + gain * b[r].astype(F32)).astype(BF)

    for cp in copies[:24]:
        cp.wait()
    cur = x[...]
    gain = gain_of(cur)
    for cp in copies[24:32]:
        cp.wait()
    multiply(cur, range(4))
    for cp in copies[32:]:
        cp.wait()
    multiply(cur, range(4, 8))
    finish(gain)

    def step(_, carry):
        cur = x[...]
        gain = gain_of(cur)
        multiply(cur, range(8))
        finish(gain)
        return carry

    lax.fori_loop(1, STEPS, step, 0)
    for k in range(8):
        outs[k][...] = x[:, k * 256:(k + 1) * 256]


def rollout(ids, pieces, members):
    return pl.pallas_call(
        rollout_kernel,
        out_shape=[jax.ShapeDtypeStruct((128, 256), BF)] * 8,
        in_specs=[pl.BlockSpec(memory_space=pltpu.SMEM)] + [pl.BlockSpec(memory_space=pl.ANY)] * 18,
        out_specs=[pl.BlockSpec(memory_space=pltpu.VMEM)] * 8,
        scratch_shapes=[
            pltpu.VMEM((8, 2048, 256), BF),
            pltpu.VMEM((128, 2048), BF),
            pltpu.VMEM((8, 128, 256), BF),
            pltpu.VMEM((8, 128, 256), BF),
            pltpu.VMEM((128, 2048), F32),
            pltpu.SemaphoreType.DMA((40,)),
        ],
        compiler_params=pltpu.CompilerParams(vmem_limit_bytes=60 * 2**20),
        cost_estimate=cost(0.05),
        name="rollout",
    )(ids, *pieces, *members)


def update_kernel(ids_ref, all_ref, fit_ref, a0, a1, a2, lo, hi, b0, b1, keep_ref, send_ref):
    first = ids_ref[2] == 0
    x = ids_ref[4]
    where = [lax.rem(x + d, 4) for d in (0, 3, 1, 2)]
    mean = jnp.sum(all_ref[...], keepdims=True).reshape(1, 1) / POP
    var = jnp.sum((all_ref[...] - mean) ** 2, keepdims=True).reshape(1, 1) / POP
    norm = (fit_ref[...] - mean) / jnp.sqrt(var + 1e-05)
    for k, a in enumerate((a0, a1, a2, lo, hi)):
        scaled = (norm * a[...].astype(F32)).astype(BF)
        n = scaled.shape[1] // 128
        row = 2 * where[min(k, 3)] + (1 if k == 4 else 0)
        for h, b in enumerate((b0, b1)):
            d = lax.dot_general(scaled, b[...], (((0,), (0,)), ((), ())), preferred_element_type=F32)
            d = d.reshape(n, 2, 64, 256).astype(BF)
            cols = slice(h * 256, (h + 1) * 256)
            keep_ref[pl.ds(row, n), :, cols] = jnp.where(first, d[:, 0], d[:, 1])
            send_ref[pl.ds(row, n), :, cols] = jnp.where(first, d[:, 1], d[:, 0])


def partial_update(ids, everyone, fitness, a, b):
    shape = jax.ShapeDtypeStruct((8, 64, 512), BF)
    return pl.pallas_call(
        update_kernel,
        out_shape=[shape, shape],
        in_specs=[pl.BlockSpec(memory_space=pltpu.SMEM)] + [pl.BlockSpec(memory_space=pltpu.VMEM)] * 9,
        out_specs=[pl.BlockSpec(memory_space=pltpu.VMEM)] * 2,
        compiler_params=pltpu.CompilerParams(vmem_limit_bytes=60 * 2**20),
        cost_estimate=cost(0.05),
        name="partial_update",
    )(ids, everyone, fitness, *a, *b)


def join_kernel(ids_ref, *refs):
    pieces, out_ref = refs[:8], refs[8]
    yl, x = ids_ref[3], ids_ref[4]
    for k, (dy, dx) in enumerate(SHIFTS):
        block = (yl if dy == 0 else 1 - yl) * 4 + lax.rem(x + dx, 4)
        out_ref[rows_of(block), :] = pieces[k][...]


def join_members(ids, pieces):
    return pl.pallas_call(
        join_kernel,
        out_shape=jax.ShapeDtypeStruct((1024, 256), BF),
        in_specs=[pl.BlockSpec(memory_space=pltpu.SMEM)] + [pl.BlockSpec(memory_space=pltpu.VMEM)] * 8,
        out_specs=pl.BlockSpec(memory_space=pltpu.VMEM),
        compiler_params=pltpu.CompilerParams(vmem_limit_bytes=60 * 2**20),
        name="join_members",
    )(ids, *pieces)


def local(states, weight, noise_in, noise_out, fitness):
    yh, z, c = (lax.axis_index(n) for n in POP_AXES)
    yl, x = (lax.axis_index(n) for n in COL_AXES)
    ids = jnp.stack([yh, z, c, yl, x]).astype(jnp.int32)

    with jax.named_scope("weight_rows"):
        share = lax.dynamic_slice_in_dim(weight, (z % 4) * 512 + c * 256, 256, 0)
        own = [jnp.stack([share] + [shift(share, "x", dx) for dx in (1, 2, 3)])]
        b = [noise_out, swap(noise_out, "yl")]

    with jax.named_scope("round_1"):
        first = own[0]
        own.append(swap(after(first, b[1]), "yl"))
        up, down = [shift(first, "z", 1)], [shift(first, "z", -1)]
        left, right = shift(noise_in, "x", 1), shift(noise_in, "x", -1)
        along_z = lax.all_to_all(jnp.broadcast_to(fitness.reshape(1, 8, 128), (8, 8, 128)), "z", 0, 0)
        parts = split_members(ids, states, noise_in, *b)
        got = over_x(after(parts, first, along_z))

    with jax.named_scope("round_2"):
        crossed_1 = [swap(after(up[0], left), "c"), swap(after(down[0], right), "c")]
        own_crossed = swap(own[1], "c")
        second, along_z = lax.optimization_barrier((own[1], along_z, own_crossed, *crossed_1))[:2]
        up.append(shift(second, "z", 1))
        down.append(shift(second, "z", -1))
        pair = jnp.stack([along_z, swap(along_z, "c")])
        everyone = jnp.stack([pair, swap(pair, "yh")]).reshape(32, 8, 128)
        others = [swap(after(own[0], got), "c"), own_crossed] + crossed_1

    with jax.named_scope("round_3"):
        fore, back = lax.optimization_barrier((up[0], down[1], up[1], everyone))[:2]
        far = [shift(fore, "z", 1), shift(back, "z", -1)]
        turned = swap(got[:, 4:], "yl")
        a = [noise_in, left, right, shift(left[:, :128], "x", 1), shift(right[:, 128:], "x", -1)]
        near = [swap(after(v, others[0]), "c") for v in (up[1], down[1])]
        keep, send = partial_update(ids, everyone, fitness.reshape(1024, 1), a, b)

    with jax.named_scope("weight"):
        last = lax.optimization_barrier((*far, *near, *others, turned))[:2]
        crossed = [swap(v, "c") for v in last]
        pieces = own + others[:2] + up + [others[2], near[0]] + down + [others[3], near[1]]
        pieces += far + crossed

    with jax.named_scope("update"):
        both = (keep.astype(F32) + swap(send, "c").astype(F32)).astype(BF)
        both = after(both, *crossed)
        stacked = lax.all_to_all(both, "z", 0, 0)
        total = jnp.sum(stacked.astype(F32), axis=0)
        left, right = total[:, :256], total[:, 256:]
        same = yh == yl
        one = jnp.where(same, left, right)
        two = jnp.where(same, right, left)
        pairs = [(i, j) for i in range(2) for j in range(2)]
        one = lax.ppermute(one, ("yh", "yl"), [(i * 2 + j, j * 2 + i) for i, j in pairs])
        two = lax.ppermute(two, ("yh", "yl"), [(i * 2 + j, j * 2 + (1 - i)) for i, j in pairs])
        update = (one + two) / jnp.sqrt(jnp.float32(POP))

    with jax.named_scope("rollout"):
        done = rollout(ids, pieces, [got, turned])
    with jax.named_scope("states_back"):
        back = [done[0]] + [col_shift(done[k], dy, -dx) for k, (dy, dx) in enumerate(SHIFTS) if k > 0]
        final = join_members(ids, back)
    return final, update


def solution(mesh):
    fine = Mesh(mesh.devices.reshape(2, 8, 2, 2, 4), POP_AXES + COL_AXES)
    both = P(POP_AXES, COL_AXES)
    return jax.shard_map(
        local,
        mesh=fine,
        in_specs=(both, P(None, COL_AXES), both, both, P(POP_AXES)),
        out_specs=(both, both),
        check_vma=False,
    )
```

```python
import jax
import jax.numpy as jnp
from jax import lax
from jax.experimental import pallas as pl
from jax.experimental.pallas import tpu as pltpu
from jax.sharding import Mesh, PartitionSpec as P

STEPS = 4
SCALE = 0.02
POP = 32768
POP_AXES = ("yh", "z", "c")
COL_AXES = ("yl", "x")
SHIFTS = [(dy, dx) for dy in range(2) for dx in range(4)]
BF = jnp.bfloat16
F32 = jnp.float32


def col_shift(v, dy, dx):
    perm = []
    for yl in range(2):
        for x in range(4):
            perm.append((yl * 4 + x, (yl ^ dy) * 4 + (x + dx) % 4))
    return lax.ppermute(v, COL_AXES, perm)


def shift(v, axis, d):
    n = 8 if axis == "z" else 4
    return lax.ppermute(v, axis, [(i, (i + d) % n) for i in range(n)])


def over_x(v):
    return lax.all_to_all(v, "x", 0, 0)


def swap(v, axis):
    return lax.ppermute(v, axis, [(0, 1), (1, 0)])


def after(v, *deps):
    return lax.optimization_barrier((v,) + deps)[0]


def rows_of(block):
    return pl.ds(pl.multiple_of(block * 128, 128), 128)


def cost(us):
    return pl.CostEstimate(flops=int(us * 1.15e9), bytes_accessed=0, transcendentals=0)


def split_kernel(ids_ref, s_ref, a_ref, b_ref, o_ref, out_ref):
    yl = ids_ref[3]
    for k in range(4):
        mine, other = rows_of(yl * 4 + k), rows_of((1 - yl) * 4 + k)
        for n, (src, rows) in enumerate(
            ((s_ref, mine), (a_ref, mine), (b_ref, mine), (o_ref, mine), (s_ref, other), (a_ref, other))
        ):
            out_ref[k, n] = src[rows, :]


def split_members(ids, states, a, b, other):
    return pl.pallas_call(
        split_kernel,
        out_shape=jax.ShapeDtypeStruct((4, 6, 128, 256), BF),
        in_specs=[pl.BlockSpec(memory_space=pltpu.SMEM)] + [pl.BlockSpec(memory_space=pltpu.VMEM)] * 4,
        out_specs=pl.BlockSpec(memory_space=pltpu.VMEM),
        compiler_params=pltpu.CompilerParams(vmem_limit_bytes=60 * 2**20),
        cost_estimate=cost(0.05),
        name="split_members",
    )(ids, states, a, b, other)


def rollout_kernel(ids_ref, *refs):
    pieces, (got, turned) = refs[:16], refs[16:18]
    outs = refs[18:26]
    w, x, a, b, pre, sem = refs[26:]
    z, c, yl, xx = ids_ref[1], ids_ref[2], ids_ref[3], ids_ref[4]
    copies = []

    def copy(src, dst):
        copies.append(pltpu.make_async_copy(src, dst, sem.at[len(copies)]))

    for k in range(4):
        r = lax.rem(xx - k + 4, 4)
        copy(got.at[k, 0], x.at[:, pl.ds(pl.multiple_of(r * 256, 256), 256)])
        copy(turned.at[k, 0], x.at[:, pl.ds(pl.multiple_of(r * 256 + 1024, 256), 256)])
        copy(got.at[k, 1], a.at[r])
        copy(turned.at[k, 1], a.at[r + 4])
        copy(got.at[k, 2], b.at[r])
        copy(got.at[k, 3], b.at[r + 4])
    for part in range(2):
        for i in range(part, 16, 2):
            d, core = (0, 1, -1, 2)[i // 4], (i // 2) % 2
            zz = lax.rem(z - d + 8, 4)
            cc = c if core == 0 else 1 - c
            r = jnp.where(zz // 2 == yl, 0, 4) + lax.rem(xx - zz * 2 - cc + 8, 4)
            copy(pieces[i], w.at[slice(4 * part, 4 * part + 4), pl.ds(pl.multiple_of(r * 256, 256), 256)])
    for cp in copies:
        cp.start()

    def multiply(cur, blocks):
        for r in blocks:
            pre[:, r * 256:(r + 1) * 256] = jnp.dot(cur, w[r], preferred_element_type=F32)

    def gain_of(cur):
        dots = jnp.zeros((128, 1), F32)
        for r in range(8):
            block = cur[:, r * 256:(r + 1) * 256].astype(F32)
            dots += jnp.sum(block * a[r].astype(F32), axis=1, keepdims=True)
        return SCALE * dots

    def finish(gain):
        for r in range(8):
            cols = slice(r * 256, (r + 1) * 256)
            x[:, cols] = jnp.tanh(pre[:, cols] + gain * b[r].astype(F32)).astype(BF)

    for cp in copies[:24]:
        cp.wait()
    cur = x[...]
    gain = gain_of(cur)
    for cp in copies[24:32]:
        cp.wait()
    multiply(cur, range(4))
    for cp in copies[32:]:
        cp.wait()
    multiply(cur, range(4, 8))
    finish(gain)

    def step(_, carry):
        cur = x[...]
        gain = gain_of(cur)
        multiply(cur, range(8))
        finish(gain)
        return carry

    lax.fori_loop(1, STEPS, step, 0)
    for k in range(8):
        outs[k][...] = x[:, k * 256:(k + 1) * 256]


def rollout(ids, pieces, members):
    return pl.pallas_call(
        rollout_kernel,
        out_shape=[jax.ShapeDtypeStruct((128, 256), BF)] * 8,
        in_specs=[pl.BlockSpec(memory_space=pltpu.SMEM)] + [pl.BlockSpec(memory_space=pl.ANY)] * 18,
        out_specs=[pl.BlockSpec(memory_space=pltpu.VMEM)] * 8,
        scratch_shapes=[
            pltpu.VMEM((8, 2048, 256), BF),
            pltpu.VMEM((128, 2048), BF),
            pltpu.VMEM((8, 128, 256), BF),
            pltpu.VMEM((8, 128, 256), BF),
            pltpu.VMEM((128, 2048), F32),
            pltpu.SemaphoreType.DMA((40,)),
        ],
        compiler_params=pltpu.CompilerParams(vmem_limit_bytes=60 * 2**20),
        cost_estimate=cost(0.05),
        name="rollout",
    )(ids, *pieces, *members)


def update_kernel(ids_ref, all_ref, fit_ref, a0, a1, a2, lo, hi, b0, b1, keep_ref, send_ref):
    first = ids_ref[2] == 0
    x = ids_ref[4]
    where = [lax.rem(x + d, 4) for d in (0, 3, 1, 2)]
    mean = jnp.sum(all_ref[...], keepdims=True).reshape(1, 1) / POP
    var = jnp.sum((all_ref[...] - mean) ** 2, keepdims=True).reshape(1, 1) / POP
    norm = (fit_ref[...] - mean) / jnp.sqrt(var + 1e-05)
    for k, a in enumerate((a0, a1, a2, lo, hi)):
        scaled = (norm * a[...].astype(F32)).astype(BF)
        n = scaled.shape[1] // 128
        row = 2 * where[min(k, 3)] + (1 if k == 4 else 0)
        for h, b in enumerate((b0, b1)):
            d = lax.dot_general(scaled, b[...], (((0,), (0,)), ((), ())), preferred_element_type=F32)
            d = d.reshape(n, 2, 64, 256).astype(BF)
            cols = slice(h * 256, (h + 1) * 256)
            keep_ref[pl.ds(row, n), :, cols] = jnp.where(first, d[:, 0], d[:, 1])
            send_ref[pl.ds(row, n), :, cols] = jnp.where(first, d[:, 1], d[:, 0])


def partial_update(ids, everyone, fitness, a, b):
    shape = jax.ShapeDtypeStruct((8, 64, 512), BF)
    return pl.pallas_call(
        update_kernel,
        out_shape=[shape, shape],
        in_specs=[pl.BlockSpec(memory_space=pltpu.SMEM)] + [pl.BlockSpec(memory_space=pltpu.VMEM)] * 9,
        out_specs=[pl.BlockSpec(memory_space=pltpu.VMEM)] * 2,
        compiler_params=pltpu.CompilerParams(vmem_limit_bytes=60 * 2**20),
        cost_estimate=cost(0.05),
        name="partial_update",
    )(ids, everyone, fitness, *a, *b)


def join_kernel(ids_ref, *refs):
    pieces, out_ref = refs[:8], refs[8]
    yl, x = ids_ref[3], ids_ref[4]
    for k, (dy, dx) in enumerate(SHIFTS):
        block = (yl if dy == 0 else 1 - yl) * 4 + lax.rem(x + dx, 4)
        out_ref[rows_of(block), :] = pieces[k][...]


def join_members(ids, pieces):
    return pl.pallas_call(
        join_kernel,
        out_shape=jax.ShapeDtypeStruct((1024, 256), BF),
        in_specs=[pl.BlockSpec(memory_space=pltpu.SMEM)] + [pl.BlockSpec(memory_space=pltpu.VMEM)] * 8,
        out_specs=pl.BlockSpec(memory_space=pltpu.VMEM),
        compiler_params=pltpu.CompilerParams(vmem_limit_bytes=60 * 2**20),
        name="join_members",
    )(ids, *pieces)


def local(states, weight, noise_in, noise_out, fitness):
    yh, z, c = (lax.axis_index(n) for n in POP_AXES)
    yl, x = (lax.axis_index(n) for n in COL_AXES)
    ids = jnp.stack([yh, z, c, yl, x]).astype(jnp.int32)

    with jax.named_scope("weight_rows"):
        share = lax.dynamic_slice_in_dim(weight, (z % 4) * 512 + c * 256, 256, 0)
        own = [jnp.stack([share] + [shift(share, "x", dx) for dx in (1, 2, 3)])]
        b = [noise_out, swap(noise_out, "yl")]

    with jax.named_scope("round_1"):
        first = own[0]
        own.append(swap(after(first, b[1]), "yl"))
        up, down = [shift(first, "z", 1)], [shift(first, "z", -1)]
        left, right = shift(noise_in, "x", 1), shift(noise_in, "x", -1)
        parts = split_members(ids, states, noise_in, *b)
        got = over_x(after(parts, first))

    with jax.named_scope("round_2"):
        crossed_1 = [swap(after(up[0], left), "c"), swap(after(down[0], right), "c")]
        own_crossed = swap(own[1], "c")
        second, pair = lax.optimization_barrier((own[1], fitness, own_crossed, *crossed_1))[:2]
        up.append(shift(second, "z", 1))
        down.append(shift(second, "z", -1))
        pair = jnp.stack([pair, swap(pair, "c")])
        four = jnp.stack([pair, swap(pair, "yh")])
        four = after(four, got)
        everyone = lax.all_to_all(jnp.broadcast_to(four.reshape(1, 32, 128), (8, 32, 128)), "z", 0, 0)
        others = [swap(after(own[0], four), "c"), own_crossed] + crossed_1

    with jax.named_scope("round_3"):
        fore, back = lax.optimization_barrier((up[0], down[1], up[1]))[:2]
        far = [shift(fore, "z", 1), shift(back, "z", -1)]
        turned = swap(got[:, 4:], "yl")
        a = [noise_in, left, right, shift(left[:, :128], "x", 1), shift(right[:, 128:], "x", -1)]
        near = [swap(after(v, others[0]), "c") for v in (up[1], down[1])]
        keep, send = partial_update(ids, everyone, fitness.reshape(1024, 1), a, b)

    with jax.named_scope("weight"):
        last = lax.optimization_barrier((*far, *near, *others, turned))[:2]
        crossed = [swap(v, "c") for v in last]
        pieces = own + others[:2] + up + [others[2], near[0]] + down + [others[3], near[1]]
        pieces += far + crossed

    with jax.named_scope("update"):
        both = (keep.astype(F32) + swap(send, "c").astype(F32)).astype(BF)
        both = after(both, *crossed)
        stacked = lax.all_to_all(both, "z", 0, 0)
        total = jnp.sum(stacked.astype(F32), axis=0)
        left, right = total[:, :256], total[:, 256:]
        same = yh == yl
        one = jnp.where(same, left, right)
        two = jnp.where(same, right, left)
        pairs = [(i, j) for i in range(2) for j in range(2)]
        one = lax.ppermute(one, ("yh", "yl"), [(i * 2 + j, j * 2 + i) for i, j in pairs])
        two = lax.ppermute(two, ("yh", "yl"), [(i * 2 + j, j * 2 + (1 - i)) for i, j in pairs])
        update = (one + two) / jnp.sqrt(jnp.float32(POP))

    with jax.named_scope("rollout"):
        done = rollout(ids, pieces, [got, turned])
    with jax.named_scope("states_back"):
        back = [done[0]] + [col_shift(done[k], dy, -dx) for k, (dy, dx) in enumerate(SHIFTS) if k > 0]
        final = join_members(ids, back)
    return final, update


def solution(mesh):
    fine = Mesh(mesh.devices.reshape(2, 8, 2, 2, 4), POP_AXES + COL_AXES)
    both = P(POP_AXES, COL_AXES)
    return jax.shard_map(
        local,
        mesh=fine,
        in_specs=(both, P(None, COL_AXES), both, both, P(POP_AXES)),
        out_specs=(both, both),
        check_vma=False,
    )
```

```python
import jax
import jax.numpy as jnp
from jax import lax
from jax.experimental import pallas as pl
from jax.experimental.pallas import tpu as pltpu
from jax.sharding import Mesh, PartitionSpec as P

STEPS = 4
SCALE = 0.02
POP = 32768
POP_AXES = ("yh", "z", "c")
COL_AXES = ("yl", "x")
SHIFTS = [(dy, dx) for dy in range(2) for dx in range(4)]
BF = jnp.bfloat16
F32 = jnp.float32


def col_shift(v, dy, dx):
    perm = []
    for yl in range(2):
        for x in range(4):
            perm.append((yl * 4 + x, (yl ^ dy) * 4 + (x + dx) % 4))
    return lax.ppermute(v, COL_AXES, perm)


def shift(v, axis, d):
    n = 8 if axis == "z" else 4
    return lax.ppermute(v, axis, [(i, (i + d) % n) for i in range(n)])


def over_x(v):
    return lax.all_to_all(v, "x", 0, 0)


def swap(v, axis):
    return lax.ppermute(v, axis, [(0, 1), (1, 0)])


def after(v, *deps):
    return lax.optimization_barrier((v,) + deps)[0]


def rows_of(block):
    return pl.ds(pl.multiple_of(block * 128, 128), 128)


def cost(us):
    return pl.CostEstimate(flops=int(us * 1.15e9), bytes_accessed=0, transcendentals=0)


def split_kernel(ids_ref, s_ref, a_ref, b_ref, o_ref, out_ref):
    yl = ids_ref[3]
    for k in range(4):
        mine, other = rows_of(yl * 4 + k), rows_of((1 - yl) * 4 + k)
        for n, (src, rows) in enumerate(
            ((s_ref, mine), (a_ref, mine), (b_ref, mine), (o_ref, mine), (s_ref, other), (a_ref, other))
        ):
            out_ref[k, n] = src[rows, :]


def split_members(ids, states, a, b, other):
    return pl.pallas_call(
        split_kernel,
        out_shape=jax.ShapeDtypeStruct((4, 6, 128, 256), BF),
        in_specs=[pl.BlockSpec(memory_space=pltpu.SMEM)] + [pl.BlockSpec(memory_space=pltpu.VMEM)] * 4,
        out_specs=pl.BlockSpec(memory_space=pltpu.VMEM),
        compiler_params=pltpu.CompilerParams(vmem_limit_bytes=60 * 2**20),
        cost_estimate=cost(0.05),
        name="split_members",
    )(ids, states, a, b, other)


def rollout_kernel(ids_ref, *refs):
    pieces, (got, turned) = refs[:16], refs[16:18]
    outs = refs[18:26]
    w, x, a, b, pre, sem = refs[26:]
    z, c, yl, xx = ids_ref[1], ids_ref[2], ids_ref[3], ids_ref[4]
    copies = []

    def copy(src, dst):
        copies.append(pltpu.make_async_copy(src, dst, sem.at[len(copies)]))

    for k in range(4):
        r = lax.rem(xx - k + 4, 4)
        copy(got.at[k, 0], x.at[:, pl.ds(pl.multiple_of(r * 256, 256), 256)])
        copy(turned.at[k, 0], x.at[:, pl.ds(pl.multiple_of(r * 256 + 1024, 256), 256)])
        copy(got.at[k, 1], a.at[r])
        copy(turned.at[k, 1], a.at[r + 4])
        copy(got.at[k, 2], b.at[r])
        copy(got.at[k, 3], b.at[r + 4])
    for part in range(2):
        for i in range(part, 16, 2):
            d, core = (0, 1, -1, 2)[i // 4], (i // 2) % 2
            zz = lax.rem(z - d + 8, 4)
            cc = c if core == 0 else 1 - c
            r = jnp.where(zz // 2 == yl, 0, 4) + lax.rem(xx - zz * 2 - cc + 8, 4)
            copy(pieces[i], w.at[slice(4 * part, 4 * part + 4), pl.ds(pl.multiple_of(r * 256, 256), 256)])
    for cp in copies:
        cp.start()

    def multiply(cur, blocks):
        for r in blocks:
            pre[:, r * 256:(r + 1) * 256] = jnp.dot(cur, w[r], preferred_element_type=F32)

    def gain_of(cur):
        dots = jnp.zeros((128, 1), F32)
        for r in range(8):
            block = cur[:, r * 256:(r + 1) * 256].astype(F32)
            dots += jnp.sum(block * a[r].astype(F32), axis=1, keepdims=True)
        return SCALE * dots

    def finish(gain):
        for r in range(8):
            cols = slice(r * 256, (r + 1) * 256)
            x[:, cols] = jnp.tanh(pre[:, cols] + gain * b[r].astype(F32)).astype(BF)

    for cp in copies[:24]:
        cp.wait()
    cur = x[...]
    gain = gain_of(cur)
    for cp in copies[24:32]:
        cp.wait()
    multiply(cur, range(4))
    for cp in copies[32:]:
        cp.wait()
    multiply(cur, range(4, 8))
    finish(gain)

    def step(_, carry):
        cur = x[...]
        gain = gain_of(cur)
        multiply(cur, range(8))
        finish(gain)
        return carry

    lax.fori_loop(1, STEPS, step, 0)
    for k in range(8):
        outs[k][...] = x[:, k * 256:(k + 1) * 256]


def rollout(ids, pieces, members):
    return pl.pallas_call(
        rollout_kernel,
        out_shape=[jax.ShapeDtypeStruct((128, 256), BF)] * 8,
        in_specs=[pl.BlockSpec(memory_space=pltpu.SMEM)] + [pl.BlockSpec(memory_space=pl.ANY)] * 18,
        out_specs=[pl.BlockSpec(memory_space=pltpu.VMEM)] * 8,
        scratch_shapes=[
            pltpu.VMEM((8, 2048, 256), BF),
            pltpu.VMEM((128, 2048), BF),
            pltpu.VMEM((8, 128, 256), BF),
            pltpu.VMEM((8, 128, 256), BF),
            pltpu.VMEM((128, 2048), F32),
            pltpu.SemaphoreType.DMA((40,)),
        ],
        compiler_params=pltpu.CompilerParams(vmem_limit_bytes=60 * 2**20),
        cost_estimate=cost(0.05),
        name="rollout",
    )(ids, *pieces, *members)


def update_kernel(ids_ref, all_ref, fit_ref, a0, a1, a2, lo, hi, b0, b1, keep_ref, send_ref):
    first = ids_ref[2] == 0
    x = ids_ref[4]
    where = [lax.rem(x + d, 4) for d in (0, 3, 1, 2)]
    mean = jnp.sum(all_ref[...], keepdims=True).reshape(1, 1) / POP
    var = jnp.sum((all_ref[...] - mean) ** 2, keepdims=True).reshape(1, 1) / POP
    norm = (fit_ref[...] - mean) / jnp.sqrt(var + 1e-05)
    for k, a in enumerate((a0, a1, a2, lo, hi)):
        scaled = (norm * a[...].astype(F32)).astype(BF)
        n = scaled.shape[1] // 128
        row = 2 * where[min(k, 3)] + (1 if k == 4 else 0)
        for h, b in enumerate((b0, b1)):
            d = lax.dot_general(scaled, b[...], (((0,), (0,)), ((), ())), preferred_element_type=F32)
            d = d.reshape(n, 2, 64, 256).astype(BF)
            cols = slice(h * 256, (h + 1) * 256)
            keep_ref[pl.ds(row, n), :, cols] = jnp.where(first, d[:, 0], d[:, 1])
            send_ref[pl.ds(row, n), :, cols] = jnp.where(first, d[:, 1], d[:, 0])


def partial_update(ids, everyone, fitness, a, b):
    shape = jax.ShapeDtypeStruct((8, 64, 512), BF)
    return pl.pallas_call(
        update_kernel,
        out_shape=[shape, shape],
        in_specs=[pl.BlockSpec(memory_space=pltpu.SMEM)] + [pl.BlockSpec(memory_space=pltpu.VMEM)] * 9,
        out_specs=[pl.BlockSpec(memory_space=pltpu.VMEM)] * 2,
        compiler_params=pltpu.CompilerParams(vmem_limit_bytes=60 * 2**20),
        cost_estimate=cost(0.05),
        name="partial_update",
    )(ids, everyone, fitness, *a, *b)


def join_kernel(ids_ref, *refs):
    pieces, out_ref = refs[:8], refs[8]
    yl, x = ids_ref[3], ids_ref[4]
    for k, (dy, dx) in enumerate(SHIFTS):
        block = (yl if dy == 0 else 1 - yl) * 4 + lax.rem(x + dx, 4)
        out_ref[rows_of(block), :] = pieces[k][...]


def join_members(ids, pieces):
    return pl.pallas_call(
        join_kernel,
        out_shape=jax.ShapeDtypeStruct((1024, 256), BF),
        in_specs=[pl.BlockSpec(memory_space=pltpu.SMEM)] + [pl.BlockSpec(memory_space=pltpu.VMEM)] * 8,
        out_specs=pl.BlockSpec(memory_space=pltpu.VMEM),
        compiler_params=pltpu.CompilerParams(vmem_limit_bytes=60 * 2**20),
        name="join_members",
    )(ids, *pieces)


def local(states, weight, noise_in, noise_out, fitness):
    yh, z, c = (lax.axis_index(n) for n in POP_AXES)
    yl, x = (lax.axis_index(n) for n in COL_AXES)
    ids = jnp.stack([yh, z, c, yl, x]).astype(jnp.int32)

    with jax.named_scope("weight_rows"):
        share = lax.dynamic_slice_in_dim(weight, (z % 4) * 512 + c * 256, 256, 0)
        own = [jnp.stack([share] + [shift(share, "x", dx) for dx in (1, 2, 3)])]
        b = [noise_out, swap(noise_out, "yl")]

    with jax.named_scope("round_1"):
        first = own[0]
        own.append(swap(after(first, b[1]), "yl"))
        up, down = [shift(first, "z", 1)], [shift(first, "z", -1)]
        left, right = shift(noise_in, "x", 1), shift(noise_in, "x", -1)
        parts = split_members(ids, states, noise_in, *b)
        got = over_x(after(parts, first))

    with jax.named_scope("round_2"):
        crossed_1 = [swap(after(up[0], left), "c"), swap(after(down[0], right), "c")]
        own_crossed = swap(own[1], "c")
        second, pair = lax.optimization_barrier((own[1], fitness, own_crossed, *crossed_1))[:2]
        up.append(shift(second, "z", 1))
        down.append(shift(second, "z", -1))
        a = [noise_in, left, right, shift(left[:, :128], "x", 1), shift(right[:, 128:], "x", -1)]
        pair = jnp.stack([pair, swap(pair, "c")])
        four = jnp.stack([pair, swap(pair, "yh")])
        four = after(four, got)
        everyone = lax.all_to_all(jnp.broadcast_to(four.reshape(1, 32, 128), (8, 32, 128)), "z", 0, 0)
        others = [swap(after(own[0], four, *a[3:]), "c"), own_crossed] + crossed_1

    with jax.named_scope("round_3"):
        fore, back = lax.optimization_barrier((up[0], down[1], up[1]))[:2]
        far = [shift(fore, "z", 1), shift(back, "z", -1)]
        turned = swap(got[:, 4:], "yl")
        near = [swap(after(v, others[0], everyone), "c") for v in (up[1], down[1])]
        keep, send = partial_update(ids, everyone, fitness.reshape(1024, 1), a, b)

    with jax.named_scope("weight"):
        last = lax.optimization_barrier((*far, *near, *others, turned))[:2]
        crossed = [swap(v, "c") for v in last]
        pieces = own + others[:2] + up + [others[2], near[0]] + down + [others[3], near[1]]
        pieces += far + crossed

    with jax.named_scope("update"):
        both = (keep.astype(F32) + swap(send, "c").astype(F32)).astype(BF)
        both = after(both, *crossed)
        stacked = lax.all_to_all(both, "z", 0, 0)
        total = jnp.sum(stacked.astype(F32), axis=0)
        left, right = total[:, :256], total[:, 256:]
        same = yh == yl
        one = jnp.where(same, left, right)
        two = jnp.where(same, right, left)
        pairs = [(i, j) for i in range(2) for j in range(2)]
        one = lax.ppermute(one, ("yh", "yl"), [(i * 2 + j, j * 2 + i) for i, j in pairs])
        two = lax.ppermute(two, ("yh", "yl"), [(i * 2 + j, j * 2 + (1 - i)) for i, j in pairs])
        update = (one + two) / jnp.sqrt(jnp.float32(POP))

    with jax.named_scope("rollout"):
        done = rollout(ids, pieces, [got, turned])
    with jax.named_scope("states_back"):
        back = [done[0]] + [col_shift(done[k], dy, -dx) for k, (dy, dx) in enumerate(SHIFTS) if k > 0]
        final = join_members(ids, back)
    return final, update


def solution(mesh):
    fine = Mesh(mesh.devices.reshape(2, 8, 2, 2, 4), POP_AXES + COL_AXES)
    both = P(POP_AXES, COL_AXES)
    return jax.shard_map(
        local,
        mesh=fine,
        in_specs=(both, P(None, COL_AXES), both, both, P(POP_AXES)),
        out_specs=(both, both),
        check_vma=False,
    )
```

```python
import jax
import jax.numpy as jnp
from jax import lax
from jax.experimental import pallas as pl
from jax.experimental.pallas import tpu as pltpu
from jax.sharding import Mesh, PartitionSpec as P

STEPS = 4
SCALE = 0.02
POP = 32768
POP_AXES = ("yh", "z", "c")
COL_AXES = ("yl", "x")
SHIFTS = [(dy, dx) for dy in range(2) for dx in range(4)]
BF = jnp.bfloat16
F32 = jnp.float32


def col_shift(v, dy, dx):
    perm = []
    for yl in range(2):
        for x in range(4):
            perm.append((yl * 4 + x, (yl ^ dy) * 4 + (x + dx) % 4))
    return lax.ppermute(v, COL_AXES, perm)


def shift(v, axis, d):
    n = 8 if axis == "z" else 4
    return lax.ppermute(v, axis, [(i, (i + d) % n) for i in range(n)])


def over_x(v):
    return lax.all_to_all(v, "x", 0, 0)


def swap(v, axis):
    return lax.ppermute(v, axis, [(0, 1), (1, 0)])


def after(v, *deps):
    return lax.optimization_barrier((v,) + deps)[0]


def rows_of(block):
    return pl.ds(pl.multiple_of(block * 128, 128), 128)


def cost(us):
    return pl.CostEstimate(flops=int(us * 1.15e9), bytes_accessed=0, transcendentals=0)


def split_kernel(ids_ref, s_ref, a_ref, b_ref, o_ref, out_ref):
    yl = ids_ref[3]
    for k in range(4):
        mine, other = rows_of(yl * 4 + k), rows_of((1 - yl) * 4 + k)
        for n, (src, rows) in enumerate(
            ((s_ref, mine), (a_ref, mine), (b_ref, mine), (o_ref, mine), (s_ref, other), (a_ref, other))
        ):
            out_ref[k, n] = src[rows, :]


def split_members(ids, states, a, b, other):
    return pl.pallas_call(
        split_kernel,
        out_shape=jax.ShapeDtypeStruct((4, 6, 128, 256), BF),
        in_specs=[pl.BlockSpec(memory_space=pltpu.SMEM)] + [pl.BlockSpec(memory_space=pltpu.VMEM)] * 4,
        out_specs=pl.BlockSpec(memory_space=pltpu.VMEM),
        compiler_params=pltpu.CompilerParams(vmem_limit_bytes=60 * 2**20),
        cost_estimate=cost(0.05),
        name="split_members",
    )(ids, states, a, b, other)


def rollout_kernel(ids_ref, *refs):
    pieces, (got, turned) = refs[:16], refs[16:18]
    outs = refs[18:26]
    w, x, a, b, sem = refs[26:]
    z, c, yl, xx = ids_ref[1], ids_ref[2], ids_ref[3], ids_ref[4]
    copies = []

    def copy(src, dst):
        copies.append(pltpu.make_async_copy(src, dst, sem.at[len(copies)]))

    for k in range(4):
        r = lax.rem(xx - k + 4, 4)
        copy(got.at[k, 0], x.at[0, :, pl.ds(pl.multiple_of(r * 256, 256), 256)])
        copy(turned.at[k, 0], x.at[0, :, pl.ds(pl.multiple_of(r * 256 + 1024, 256), 256)])
        copy(got.at[k, 1], a.at[r])
        copy(turned.at[k, 1], a.at[r + 4])
        copy(got.at[k, 2], b.at[r])
        copy(got.at[k, 3], b.at[r + 4])
    for part in range(2):
        for i in range(part, 16, 2):
            d, core = (0, 1, -1, 2)[i // 4], (i // 2) % 2
            zz = lax.rem(z - d + 8, 4)
            cc = c if core == 0 else 1 - c
            r = jnp.where(zz // 2 == yl, 0, 4) + lax.rem(xx - zz * 2 - cc + 8, 4)
            copy(pieces[i], w.at[slice(4 * part, 4 * part + 4), pl.ds(pl.multiple_of(r * 256, 256), 256)])
    for cp in copies:
        cp.start()

    def block(source, r, gain, target):
        pre = jnp.dot(x[source], w[r], preferred_element_type=F32)
        state = jnp.tanh(pre + gain * b[r].astype(F32)).astype(BF)
        x[target, :, r * 256:(r + 1) * 256] = state
        return jnp.sum(state.astype(F32) * a[r].astype(F32), axis=1, keepdims=True)

    for cp in copies[:24]:
        cp.wait()
    dots = jnp.zeros((128, 1), F32)
    for r in range(8):
        state = x[0, :, r * 256:(r + 1) * 256].astype(F32)
        dots += jnp.sum(state * a[r].astype(F32), axis=1, keepdims=True)
    gain, dots = SCALE * dots, jnp.zeros((128, 1), F32)
    for cp in copies[24:32]:
        cp.wait()
    for r in range(4):
        dots += block(0, r, gain, 1)
    for cp in copies[32:]:
        cp.wait()
    for r in range(4, 8):
        dots += block(0, r, gain, 1)

    def step(s, dots):
        source = lax.rem(s, 2)
        gain, dots = SCALE * dots, jnp.zeros((128, 1), F32)
        for r in range(8):
            dots += block(source, r, gain, 1 - source)
        return dots

    lax.fori_loop(1, STEPS, step, dots)
    for k in range(8):
        outs[k][...] = x[STEPS % 2, :, k * 256:(k + 1) * 256]


def rollout(ids, pieces, members):
    return pl.pallas_call(
        rollout_kernel,
        out_shape=[jax.ShapeDtypeStruct((128, 256), BF)] * 8,
        in_specs=[pl.BlockSpec(memory_space=pltpu.SMEM)] + [pl.BlockSpec(memory_space=pl.ANY)] * 18,
        out_specs=[pl.BlockSpec(memory_space=pltpu.VMEM)] * 8,
        scratch_shapes=[
            pltpu.VMEM((8, 2048, 256), BF),
            pltpu.VMEM((2, 128, 2048), BF),
            pltpu.VMEM((8, 128, 256), BF),
            pltpu.VMEM((8, 128, 256), BF),
            pltpu.SemaphoreType.DMA((40,)),
        ],
        compiler_params=pltpu.CompilerParams(vmem_limit_bytes=60 * 2**20),
        cost_estimate=cost(0.05),
        name="rollout",
    )(ids, *pieces, *members)


def update_kernel(ids_ref, all_ref, fit_ref, a0, a1, a2, lo, hi, b0, b1, keep_ref, send_ref):
    first = ids_ref[2] == 0
    x = ids_ref[4]
    where = [lax.rem(x + d, 4) for d in (0, 3, 1, 2)]
    mean = jnp.sum(all_ref[...], keepdims=True).reshape(1, 1) / POP
    var = jnp.sum((all_ref[...] - mean) ** 2, keepdims=True).reshape(1, 1) / POP
    norm = (fit_ref[...] - mean) / jnp.sqrt(var + 1e-05)
    for k, a in enumerate((a0, a1, a2, lo, hi)):
        scaled = (norm * a[...].astype(F32)).astype(BF)
        n = scaled.shape[1] // 128
        row = 2 * where[min(k, 3)] + (1 if k == 4 else 0)
        for h, b in enumerate((b0, b1)):
            d = lax.dot_general(scaled, b[...], (((0,), (0,)), ((), ())), preferred_element_type=F32)
            d = d.reshape(n, 2, 64, 256).astype(BF)
            cols = slice(h * 256, (h + 1) * 256)
            keep_ref[pl.ds(row, n), :, cols] = jnp.where(first, d[:, 0], d[:, 1])
            send_ref[pl.ds(row, n), :, cols] = jnp.where(first, d[:, 1], d[:, 0])


def partial_update(ids, everyone, fitness, a, b):
    shape = jax.ShapeDtypeStruct((8, 64, 512), BF)
    return pl.pallas_call(
        update_kernel,
        out_shape=[shape, shape],
        in_specs=[pl.BlockSpec(memory_space=pltpu.SMEM)] + [pl.BlockSpec(memory_space=pltpu.VMEM)] * 9,
        out_specs=[pl.BlockSpec(memory_space=pltpu.VMEM)] * 2,
        compiler_params=pltpu.CompilerParams(vmem_limit_bytes=60 * 2**20),
        cost_estimate=cost(0.05),
        name="partial_update",
    )(ids, everyone, fitness, *a, *b)


def join_kernel(ids_ref, *refs):
    pieces, out_ref = refs[:8], refs[8]
    yl, x = ids_ref[3], ids_ref[4]
    for k, (dy, dx) in enumerate(SHIFTS):
        block = (yl if dy == 0 else 1 - yl) * 4 + lax.rem(x + dx, 4)
        out_ref[rows_of(block), :] = pieces[k][...]


def join_members(ids, pieces):
    return pl.pallas_call(
        join_kernel,
        out_shape=jax.ShapeDtypeStruct((1024, 256), BF),
        in_specs=[pl.BlockSpec(memory_space=pltpu.SMEM)] + [pl.BlockSpec(memory_space=pltpu.VMEM)] * 8,
        out_specs=pl.BlockSpec(memory_space=pltpu.VMEM),
        compiler_params=pltpu.CompilerParams(vmem_limit_bytes=60 * 2**20),
        name="join_members",
    )(ids, *pieces)


def local(states, weight, noise_in, noise_out, fitness):
    yh, z, c = (lax.axis_index(n) for n in POP_AXES)
    yl, x = (lax.axis_index(n) for n in COL_AXES)
    ids = jnp.stack([yh, z, c, yl, x]).astype(jnp.int32)

    with jax.named_scope("weight_rows"):
        share = lax.dynamic_slice_in_dim(weight, (z % 4) * 512 + c * 256, 256, 0)
        own = [jnp.stack([share] + [shift(share, "x", dx) for dx in (1, 2, 3)])]
        b = [noise_out, swap(noise_out, "yl")]

    with jax.named_scope("round_1"):
        first = own[0]
        own.append(swap(after(first, b[1]), "yl"))
        up, down = [shift(first, "z", 1)], [shift(first, "z", -1)]
        left, right = shift(noise_in, "x", 1), shift(noise_in, "x", -1)
        parts = split_members(ids, states, noise_in, *b)
        got = over_x(after(parts, first))

    with jax.named_scope("round_2"):
        crossed_1 = [swap(after(up[0], left), "c"), swap(after(down[0], right), "c")]
        own_crossed = swap(own[1], "c")
        second, pair = lax.optimization_barrier((own[1], fitness, own_crossed, *crossed_1))[:2]
        up.append(shift(second, "z", 1))
        down.append(shift(second, "z", -1))
        a = [noise_in, left, right, shift(left[:, :128], "x", 1), shift(right[:, 128:], "x", -1)]
        pair = jnp.stack([pair, swap(pair, "c")])
        four = jnp.stack([pair, swap(pair, "yh")])
        four = after(four, got)
        everyone = lax.all_to_all(jnp.broadcast_to(four.reshape(1, 32, 128), (8, 32, 128)), "z", 0, 0)
        others = [swap(after(own[0], four, *a[3:]), "c"), own_crossed] + crossed_1

    with jax.named_scope("round_3"):
        fore, back = lax.optimization_barrier((up[0], down[1], up[1]))[:2]
        far = [shift(fore, "z", 1), shift(back, "z", -1)]
        turned = swap(got[:, 4:], "yl")
        near = [swap(after(v, others[0], everyone), "c") for v in (up[1], down[1])]
        keep, send = partial_update(ids, everyone, fitness.reshape(1024, 1), a, b)

    with jax.named_scope("weight"):
        last = lax.optimization_barrier((*far, *near, *others, turned))[:2]
        crossed = [swap(v, "c") for v in last]
        pieces = own + others[:2] + up + [others[2], near[0]] + down + [others[3], near[1]]
        pieces += far + crossed

    with jax.named_scope("update"):
        both = (keep.astype(F32) + swap(send, "c").astype(F32)).astype(BF)
        both = after(both, *crossed)
        stacked = lax.all_to_all(both, "z", 0, 0)
        total = jnp.sum(stacked.astype(F32), axis=0)
        left, right = total[:, :256], total[:, 256:]
        same = yh == yl
        one = jnp.where(same, left, right)
        two = jnp.where(same, right, left)
        pairs = [(i, j) for i in range(2) for j in range(2)]
        one = lax.ppermute(one, ("yh", "yl"), [(i * 2 + j, j * 2 + i) for i, j in pairs])
        two = lax.ppermute(two, ("yh", "yl"), [(i * 2 + j, j * 2 + (1 - i)) for i, j in pairs])
        update = (one + two) / jnp.sqrt(jnp.float32(POP))

    with jax.named_scope("rollout"):
        done = rollout(ids, pieces, [got, turned])
    with jax.named_scope("states_back"):
        back = [done[0]] + [col_shift(done[k], dy, -dx) for k, (dy, dx) in enumerate(SHIFTS) if k > 0]
        final = join_members(ids, back)
    return final, update


def solution(mesh):
    fine = Mesh(mesh.devices.reshape(2, 8, 2, 2, 4), POP_AXES + COL_AXES)
    both = P(POP_AXES, COL_AXES)
    return jax.shard_map(
        local,
        mesh=fine,
        in_specs=(both, P(None, COL_AXES), both, both, P(POP_AXES)),
        out_specs=(both, both),
        check_vma=False,
    )
```

```python
import jax
import jax.numpy as jnp
from jax import lax
from jax.experimental import pallas as pl
from jax.experimental.pallas import tpu as pltpu
from jax.sharding import Mesh, PartitionSpec as P

STEPS = 4
SCALE = 0.02
POP = 32768
POP_AXES = ("yh", "z", "c")
COL_AXES = ("yl", "x")
SHIFTS = [(dy, dx) for dy in range(2) for dx in range(4)]
BF = jnp.bfloat16
F32 = jnp.float32


def col_shift(v, dy, dx):
    perm = []
    for yl in range(2):
        for x in range(4):
            perm.append((yl * 4 + x, (yl ^ dy) * 4 + (x + dx) % 4))
    return lax.ppermute(v, COL_AXES, perm)


def shift(v, axis, d):
    n = 8 if axis == "z" else 4
    return lax.ppermute(v, axis, [(i, (i + d) % n) for i in range(n)])


def over_x(v):
    return lax.all_to_all(v, "x", 0, 0)


def swap(v, axis):
    return lax.ppermute(v, axis, [(0, 1), (1, 0)])


def after(v, *deps):
    return lax.optimization_barrier((v,) + deps)[0]


def rows_of(block):
    return pl.ds(pl.multiple_of(block * 128, 128), 128)


def cost(us):
    return pl.CostEstimate(flops=int(us * 1.15e9), bytes_accessed=0, transcendentals=0)


def split_kernel(ids_ref, s_ref, a_ref, b_ref, o_ref, out_ref):
    yl = ids_ref[3]
    for k in range(4):
        mine, other = rows_of(yl * 4 + k), rows_of((1 - yl) * 4 + k)
        for n, (src, rows) in enumerate(
            ((s_ref, mine), (a_ref, mine), (b_ref, mine), (o_ref, mine), (s_ref, other), (a_ref, other))
        ):
            out_ref[k, n] = src[rows, :]


def split_members(ids, states, a, b, other):
    return pl.pallas_call(
        split_kernel,
        out_shape=jax.ShapeDtypeStruct((4, 6, 128, 256), BF),
        in_specs=[pl.BlockSpec(memory_space=pltpu.SMEM)] + [pl.BlockSpec(memory_space=pltpu.VMEM)] * 4,
        out_specs=pl.BlockSpec(memory_space=pltpu.VMEM),
        compiler_params=pltpu.CompilerParams(vmem_limit_bytes=60 * 2**20),
        cost_estimate=cost(0.05),
        name="split_members",
    )(ids, states, a, b, other)


def rollout_kernel(ids_ref, *refs):
    pieces, (got, turned) = refs[:16], refs[16:18]
    outs = refs[18:26]
    w, x, a, b, pre, sem = refs[26:]
    z, c, yl, xx = ids_ref[1], ids_ref[2], ids_ref[3], ids_ref[4]
    copies = []

    def copy(src, dst):
        copies.append(pltpu.make_async_copy(src, dst, sem.at[len(copies)]))

    for k in range(4):
        r = lax.rem(xx - k + 4, 4)
        copy(got.at[k, 0], x.at[:, pl.ds(pl.multiple_of(r * 256, 256), 256)])
        copy(turned.at[k, 0], x.at[:, pl.ds(pl.multiple_of(r * 256 + 1024, 256), 256)])
        copy(got.at[k, 1], a.at[r])
        copy(turned.at[k, 1], a.at[r + 4])
        copy(got.at[k, 2], b.at[r])
        copy(got.at[k, 3], b.at[r + 4])
    for part in range(2):
        for i in range(part, 16, 2):
            d, core = (0, 1, -1, 2)[i // 4], (i // 2) % 2
            zz = lax.rem(z - d + 8, 4)
            cc = c if core == 0 else 1 - c
            r = jnp.where(zz // 2 == yl, 0, 4) + lax.rem(xx - zz * 2 - cc + 8, 4)
            copy(pieces[i], w.at[slice(4 * part, 4 * part + 4), pl.ds(pl.multiple_of(r * 256, 256), 256)])
    for cp in copies:
        cp.start()

    def multiply(cur, blocks):
        for r in blocks:
            pre[:, r * 256:(r + 1) * 256] = jnp.dot(cur, w[r], preferred_element_type=F32)

    def gain_of(cur):
        dots = jnp.zeros((128, 1), F32)
        for r in range(8):
            block = cur[:, r * 256:(r + 1) * 256].astype(F32)
            dots += jnp.sum(block * a[r].astype(F32), axis=1, keepdims=True)
        return SCALE * dots

    def finish(gain):
        dots = jnp.zeros((128, 1), F32)
        for r in range(8):
            cols = slice(r * 256, (r + 1) * 256)
            state = jnp.tanh(pre[:, cols] + gain * b[r].astype(F32)).astype(BF)
            x[:, cols] = state
            dots += jnp.sum(state.astype(F32) * a[r].astype(F32), axis=1, keepdims=True)
        return SCALE * dots

    for cp in copies[:24]:
        cp.wait()
    cur = x[...]
    gain = gain_of(cur)
    for cp in copies[24:32]:
        cp.wait()
    multiply(cur, range(4))
    for cp in copies[32:]:
        cp.wait()
    multiply(cur, range(4, 8))
    gain = finish(gain)

    def step(_, gain):
        multiply(x[...], range(8))
        return finish(gain)

    lax.fori_loop(1, STEPS, step, gain)
    for k in range(8):
        outs[k][...] = x[:, k * 256:(k + 1) * 256]


def rollout(ids, pieces, members):
    return pl.pallas_call(
        rollout_kernel,
        out_shape=[jax.ShapeDtypeStruct((128, 256), BF)] * 8,
        in_specs=[pl.BlockSpec(memory_space=pltpu.SMEM)] + [pl.BlockSpec(memory_space=pl.ANY)] * 18,
        out_specs=[pl.BlockSpec(memory_space=pltpu.VMEM)] * 8,
        scratch_shapes=[
            pltpu.VMEM((8, 2048, 256), BF),
            pltpu.VMEM((128, 2048), BF),
            pltpu.VMEM((8, 128, 256), BF),
            pltpu.VMEM((8, 128, 256), BF),
            pltpu.VMEM((128, 2048), F32),
            pltpu.SemaphoreType.DMA((40,)),
        ],
        compiler_params=pltpu.CompilerParams(vmem_limit_bytes=60 * 2**20),
        cost_estimate=cost(0.05),
        name="rollout",
    )(ids, *pieces, *members)


def update_kernel(ids_ref, all_ref, fit_ref, a0, a1, a2, lo, hi, b0, b1, keep_ref, send_ref):
    first = ids_ref[2] == 0
    x = ids_ref[4]
    where = [lax.rem(x + d, 4) for d in (0, 3, 1, 2)]
    mean = jnp.sum(all_ref[...], keepdims=True).reshape(1, 1) / POP
    var = jnp.sum((all_ref[...] - mean) ** 2, keepdims=True).reshape(1, 1) / POP
    norm = (fit_ref[...] - mean) / jnp.sqrt(var + 1e-05)
    for k, a in enumerate((a0, a1, a2, lo, hi)):
        scaled = (norm * a[...].astype(F32)).astype(BF)
        n = scaled.shape[1] // 128
        row = 2 * where[min(k, 3)] + (1 if k == 4 else 0)
        for h, b in enumerate((b0, b1)):
            d = lax.dot_general(scaled, b[...], (((0,), (0,)), ((), ())), preferred_element_type=F32)
            d = d.reshape(n, 2, 64, 256).astype(BF)
            cols = slice(h * 256, (h + 1) * 256)
            keep_ref[pl.ds(row, n), :, cols] = jnp.where(first, d[:, 0], d[:, 1])
            send_ref[pl.ds(row, n), :, cols] = jnp.where(first, d[:, 1], d[:, 0])


def partial_update(ids, everyone, fitness, a, b):
    shape = jax.ShapeDtypeStruct((8, 64, 512), BF)
    return pl.pallas_call(
        update_kernel,
        out_shape=[shape, shape],
        in_specs=[pl.BlockSpec(memory_space=pltpu.SMEM)] + [pl.BlockSpec(memory_space=pltpu.VMEM)] * 9,
        out_specs=[pl.BlockSpec(memory_space=pltpu.VMEM)] * 2,
        compiler_params=pltpu.CompilerParams(vmem_limit_bytes=60 * 2**20),
        cost_estimate=cost(0.05),
        name="partial_update",
    )(ids, everyone, fitness, *a, *b)


def join_kernel(ids_ref, *refs):
    pieces, out_ref = refs[:8], refs[8]
    yl, x = ids_ref[3], ids_ref[4]
    for k, (dy, dx) in enumerate(SHIFTS):
        block = (yl if dy == 0 else 1 - yl) * 4 + lax.rem(x + dx, 4)
        out_ref[rows_of(block), :] = pieces[k][...]


def join_members(ids, pieces):
    return pl.pallas_call(
        join_kernel,
        out_shape=jax.ShapeDtypeStruct((1024, 256), BF),
        in_specs=[pl.BlockSpec(memory_space=pltpu.SMEM)] + [pl.BlockSpec(memory_space=pltpu.VMEM)] * 8,
        out_specs=pl.BlockSpec(memory_space=pltpu.VMEM),
        compiler_params=pltpu.CompilerParams(vmem_limit_bytes=60 * 2**20),
        name="join_members",
    )(ids, *pieces)


def local(states, weight, noise_in, noise_out, fitness):
    yh, z, c = (lax.axis_index(n) for n in POP_AXES)
    yl, x = (lax.axis_index(n) for n in COL_AXES)
    ids = jnp.stack([yh, z, c, yl, x]).astype(jnp.int32)

    with jax.named_scope("weight_rows"):
        share = lax.dynamic_slice_in_dim(weight, (z % 4) * 512 + c * 256, 256, 0)
        own = [jnp.stack([share] + [shift(share, "x", dx) for dx in (1, 2, 3)])]
        b = [noise_out, swap(noise_out, "yl")]

    with jax.named_scope("round_1"):
        first = own[0]
        own.append(swap(after(first, b[1]), "yl"))
        up, down = [shift(first, "z", 1)], [shift(first, "z", -1)]
        left, right = shift(noise_in, "x", 1), shift(noise_in, "x", -1)
        parts = split_members(ids, states, noise_in, *b)
        got = over_x(after(parts, first))

    with jax.named_scope("round_2"):
        crossed_1 = [swap(after(up[0], left), "c"), swap(after(down[0], right), "c")]
        own_crossed = swap(own[1], "c")
        second, pair = lax.optimization_barrier((own[1], fitness, own_crossed, *crossed_1))[:2]
        up.append(shift(second, "z", 1))
        down.append(shift(second, "z", -1))
        a = [noise_in, left, right, shift(left[:, :128], "x", 1), shift(right[:, 128:], "x", -1)]
        pair = jnp.stack([pair, swap(pair, "c")])
        four = jnp.stack([pair, swap(pair, "yh")])
        four = after(four, got)
        everyone = lax.all_to_all(jnp.broadcast_to(four.reshape(1, 32, 128), (8, 32, 128)), "z", 0, 0)
        others = [swap(after(own[0], four, *a[3:]), "c"), own_crossed] + crossed_1

    with jax.named_scope("round_3"):
        fore, back = lax.optimization_barrier((up[0], down[1], up[1]))[:2]
        far = [shift(fore, "z", 1), shift(back, "z", -1)]
        turned = swap(got[:, 4:], "yl")
        near = [swap(after(v, others[0], everyone), "c") for v in (up[1], down[1])]
        keep, send = partial_update(ids, everyone, fitness.reshape(1024, 1), a, b)

    with jax.named_scope("weight"):
        last = lax.optimization_barrier((*far, *near, *others, turned))[:2]
        crossed = [swap(v, "c") for v in last]
        pieces = own + others[:2] + up + [others[2], near[0]] + down + [others[3], near[1]]
        pieces += far + crossed

    with jax.named_scope("update"):
        both = (keep.astype(F32) + swap(send, "c").astype(F32)).astype(BF)
        both = after(both, *crossed)
        stacked = lax.all_to_all(both, "z", 0, 0)
        total = jnp.sum(stacked.astype(F32), axis=0)
        left, right = total[:, :256], total[:, 256:]
        same = yh == yl
        one = jnp.where(same, left, right)
        two = jnp.where(same, right, left)
        pairs = [(i, j) for i in range(2) for j in range(2)]
        one = lax.ppermute(one, ("yh", "yl"), [(i * 2 + j, j * 2 + i) for i, j in pairs])
        two = lax.ppermute(two, ("yh", "yl"), [(i * 2 + j, j * 2 + (1 - i)) for i, j in pairs])
        update = (one + two) / jnp.sqrt(jnp.float32(POP))

    with jax.named_scope("rollout"):
        done = rollout(ids, pieces, [got, turned])
    with jax.named_scope("states_back"):
        back = [done[0]] + [col_shift(done[k], dy, -dx) for k, (dy, dx) in enumerate(SHIFTS) if k > 0]
        final = join_members(ids, back)
    return final, update


def solution(mesh):
    fine = Mesh(mesh.devices.reshape(2, 8, 2, 2, 4), POP_AXES + COL_AXES)
    both = P(POP_AXES, COL_AXES)
    return jax.shard_map(
        local,
        mesh=fine,
        in_specs=(both, P(None, COL_AXES), both, both, P(POP_AXES)),
        out_specs=(both, both),
        check_vma=False,
    )
```
